256 devices in a mesh: expert: 16 (over x_hi, y, core), cuts: 16 (over z, x_lo).
Axes of the slice: x: 4 (x_hi: 2, x_lo: 2; x = x_hi * 2 + x_lo), y: 4, z: 8, core: 2. Of those that a mesh axis runs over, the one named last changes fastest.
Arguments:
- tokens: bfloat16 [2048, 6144], P('expert'), may hold values from -6 to 6
- routes: int32 [2048, 4], P('expert'), may hold values from 0 to 15, all different within a row; in each aligned block of 128 rows (0 to 127, 128 to 255, ...) at most 64 rows name the same one
- route_weights: float32 [2048, 4], P('expert'), may hold values from 0.1 to 1
- w_gate: bfloat16 [16, 5376, 6144], P('expert', 'cuts'), may hold values from -0.078125 to 0.078125
- w_down: bfloat16 [16, 5376, 6144], P('expert', 'cuts'), may hold values from -0.078125 to 0.078125
Outputs:
- mixed: bfloat16 [2048, 6144], P('expert')
The draws below stay inside these ranges and needn't reach their ends.
Inputs may be any that keep to these rules, and one draw needn't show every extreme that they name: `routes`: each row names 4 different experts. In each aligned block of 128 rows (the rows of one index of expert) no expert is named by more than 64 rows, a bound that some block reaches.
All inputs are finite; a program needn't handle non-finite values.
Results may differ from the reference program's by a relative error of at most 0.025.
Values may be sent and summed in bfloat16 or wider, within the bound.
A program may use at most 64 MiB of HBM per device.

```python
import math
import jax
import jax.numpy as jnp
import numpy as np
from jax import lax

D = 6144
FF = 5376
TOPK = 4
TOK_DEV = 128
EXPERTS = 16
CUTS = 16
FF_BLOCK = 336
CAP = 64
TOKENS = 2048


def levels(key, extent, shards, smallest, largest):
    def one(axis_at, blocks):
        steps = jax.random.uniform(jax.random.fold_in(jax.random.fold_in(key, 6), axis_at), (blocks,), jnp.float32, smallest / len(shards), largest / len(shards))
        return jnp.repeat(jnp.exp(steps), extent[axis_at] // blocks).reshape((-1,) + (1,) * (len(extent) - axis_at - 1))

    level = one(*shards[0])
    for cut in shards[1:]:
        level = level * one(*cut)
    return level


def deal_out(stream_key, own, number, rows, amount, top, bound, slope):
    ranking = jax.random.permutation(stream_key, amount)
    crowded, ordinary = load_shares(amount, rows * top, bound, slope, True), load_shares(amount, rows * top, bound, slope, False)
    places = jnp.arange(amount)

    def named(lengths, rotation):
        used = int((lengths > 0).sum())
        fixed = max(1, used // 4)
        moved = fixed + (places - fixed + rotation * (used - fixed)) % max(1, amount - fixed)
        return jnp.zeros((amount,), jnp.int32).at[ranking[jnp.where(places < fixed, places, moved)]].set(jnp.asarray(lengths, jnp.int32))

    lengths = jnp.where(number % 4 == 0, named(crowded, number // 4), named(ordinary, number - number // 4 - 1))
    mixed = jax.random.permutation(jax.random.fold_in(own, 3), amount)
    giver, receiver = mixed[0:amount // 2 * 2:2], mixed[1:amount // 2 * 2:2]
    room = jnp.minimum(lengths[giver] - 1, bound - lengths[receiver]) // 2
    room = jnp.where((giver == ranking[0]) | (receiver == ranking[0]) | (lengths[receiver] == 0), 0, jnp.maximum(room, 0))
    moved = jax.random.randint(jax.random.fold_in(own, 4), (amount // 2,), 0, 1 << 20) % (room + 1)
    lengths = lengths.at[giver].add(-moved).at[receiver].add(moved)
    items = jnp.searchsorted(jnp.cumsum(lengths), jnp.arange(rows * top), side="right").astype(jnp.int32)
    listing = items.reshape(top, rows).T
    listing = listing[jax.random.permutation(jax.random.fold_in(own, 1), rows)]
    rotation = jax.random.randint(jax.random.fold_in(own, 2), (rows, 1), 0, top)
    return jnp.take_along_axis(listing, (jnp.arange(top)[None, :] + rotation) % top, axis=1)


def load_shares(count, total, bound, skew, full):
    portions = [(1 << 20) // math.isqrt(rank ** skew) + 1 for rank in range(1, count + 1)]
    largest = bound if full else min(bound, max(-(-total // count), total * portions[0] // sum(portions)))
    least = 1 if total - largest >= count - 1 else 0
    counts, surplus = [largest] + [least] * (count - 1), total - largest - least * (count - 1)
    while surplus > 0:
        free = [i for i in range(1, count) if counts[i] < largest] or [i for i in range(1, count) if counts[i] < bound]
        mass, remaining = sum([portions[i] for i in free]), surplus
        for i in free:
            addition = min(bound - counts[i], max(1, remaining * portions[i] // mass), surplus)
            counts[i] = counts[i] + addition
            surplus = surplus - addition
    return np.array(counts)


def bell_draw(key, extent, spread, most, cuts=(), kind=jnp.bfloat16):
    loudness = levels(key, extent, cuts, -0.22, 0.18) if cuts else 1.0
    values = jax.random.normal(key, extent, jnp.float32) * spread * loudness
    return jnp.minimum(jnp.maximum(values, -most), most).astype(kind)


def setup_inputs(seed: int = 0) -> dict:
    splits = jax.random.split(jax.random.key(seed), 6)
    tokens = bell_draw(splits[0], (TOKENS, D), 1.0, 6.0, ((0, 16),))
    routes_keys = jax.random.split(jax.random.fold_in(splits[1], 1), TOKENS // TOK_DEV)
    routes_turns = jax.random.permutation(jax.random.fold_in(splits[1], 3), TOKENS // TOK_DEV)
    routes = jax.vmap(lambda own, number: deal_out(jax.random.fold_in(splits[1], 2), own, number, TOK_DEV, EXPERTS, TOPK, CAP, 1))(routes_keys, routes_turns).reshape((TOKENS, TOPK))
    route_weights = jnp.clip(0.1 + 0.9 * jax.random.uniform(splits[2], (TOKENS, TOPK), jnp.float32) ** levels(splits[2], (TOKENS, TOPK), ((0, 16),), -0.2, 0.2), 0.1, 1.0)
    w_gate = bell_draw(splits[3], (EXPERTS, FF, D), D ** -0.5, 0.078125, ((0, 16), (1, 16)))
    w_down = bell_draw(splits[4], (EXPERTS, FF, D), FF ** -0.5, 0.078125, ((0, 16), (1, 16)))
    return dict(tokens=tokens, routes=routes, route_weights=route_weights, w_gate=w_gate, w_down=w_down)


def reference(tokens, routes, route_weights, w_gate, w_down):
    pairs = TOKENS * TOPK
    row_count = EXPERTS * CAP
    flat_ids = routes.reshape(pairs)
    flat_weights = route_weights.reshape(pairs).astype(jnp.float32)
    owner_token = (jnp.arange(pairs, dtype=jnp.int32) // TOPK).astype(jnp.int32)

    def per_expert(total, inputs):
        expert, gate_rows, down_rows = inputs
        hit_mask = flat_ids == expert
        slot_rank = (jnp.cumsum(hit_mask.astype(jnp.int32)) - 1).astype(jnp.int32)
        where_to = jnp.where(hit_mask, slot_rank, row_count).astype(jnp.int32)
        picks = jnp.zeros((row_count,), jnp.int32).at[where_to].set(owner_token, mode="drop")
        gathered = tokens[picks]
        pre_act = jnp.dot(gathered, gate_rows.T, preferred_element_type=jnp.float32)
        hidden = jax.nn.silu(pre_act).astype(jnp.bfloat16)
        hidden_blocks = hidden.reshape(row_count, CUTS, FF_BLOCK).transpose(1, 0, 2)
        down_blocks = down_rows.reshape(CUTS, FF_BLOCK, D)

        def add_block(running, pieces):
            hid_rows, down_part = pieces
            part = jnp.dot(hid_rows, down_part, preferred_element_type=jnp.float32).astype(jnp.bfloat16)
            return running + lax.optimization_barrier(part).astype(jnp.float32), None

        summed, _ = lax.scan(add_block, jnp.zeros((row_count, D), jnp.float32), (hidden_blocks, down_blocks))
        expert_out = summed.astype(jnp.bfloat16)
        picked = expert_out[jnp.clip(slot_rank, 0, row_count - 1)].astype(jnp.float32)
        weight = jnp.where(hit_mask, flat_weights, jnp.zeros_like(flat_weights))
        return total + (weight[:, None] * picked).reshape(TOKENS, TOPK, D).sum(1), None

    total, _ = lax.scan(per_expert, jnp.zeros((TOKENS, D), jnp.float32),
                        (jnp.arange(EXPERTS, dtype=jnp.int32), w_gate, w_down))
    return total.astype(jnp.bfloat16)
```

```python
import functools
import jax
import jax.numpy as jnp
from jax import lax
from jax.experimental import pallas as pl
from jax.experimental.pallas import tpu as pltpu
from jax.sharding import PartitionSpec as P

MESH = pl.DeviceIdType.MESH
BF = jnp.bfloat16
F32 = jnp.float32

D = 6144
FF = 336
FF2 = 2 * FF
ROWS = 128
EXPERTS = 16
NS = 12
CW = D // NS
HW = CW // 2
ZP = 4
NI = 2 * NS // 2 - ZP
NP = NS // 2


def kernel(
    wt_ref, tok_ref, wg_ref, wd_ref, o_ref,
    xp, wg, wd, pre, hid, wt,
    ry1, ry2, rx1, rx2, qx1, qx2, qy1, qy2, tz, fz,
    tok_sem, wgo, wgs, wgr, wdo, wds, wdr, wts, wtr,
    s1s, s1r, s2s, s2r, s3s, s3r, s4s, s4r, s5s, s5r,
    y1s, y1r, y2s, y2r, x1s, x1r, x2s, x2r,
    u1s, u1r, u2s, u2r, v1s, v1r, v2s, v2r,
    z1s, z1r, ags, agr, aglo,
):
    e = lax.axis_index("expert")
    c = lax.axis_index("cuts")
    hi, y, k = e // 8, (e // 2) % 4, e % 2
    z, lo = c // 2, c % 2
    ol = 1 - lo

    def dev(hi_, y_, k_, z_, lo_):
        return (hi_ * 8 + y_ * 2 + k_, z_ * 2 + lo_)

    yp = dev(hi, (y + 1) % 4, k, z, lo)
    ym = dev(hi, (y + 3) % 4, k, z, lo)
    inner = dev(hi, y, k, z, ol)
    outer = dev(1 - hi, y, k, z, ol)
    core = dev(hi, y, 1 - k, z, lo)

    def zdev(dz, lo_):
        return dev(hi, y, k, (z + dz) % 8, lo_)

    def rel(dx, dy):
        if dx == 0:
            return dev(hi, (y + dy) % 4, k, z, lo)
        return dev(1 - hi, (y + dy) % 4, k, z, ol)

    def remote(src, dst, ss, rs, to):
        return pltpu.make_async_remote_copy(
            src_ref=src, dst_ref=dst, send_sem=ss, recv_sem=rs, device_id=to, device_id_type=MESH
        )

    def load_tok(s, h):
        return pltpu.make_async_copy(
            tok_ref.at[:, pl.ds(pl.multiple_of(s * CW + h * HW, HW), HW)],
            xp.at[s, h, 0, 0], tok_sem.at[s, h],
        )

    def cols(s):
        return pl.ds(pl.multiple_of(s * CW, CW), CW)

    def load_w(src, dst, sem, s):
        return pltpu.make_async_copy(src.at[0, :, cols(s)], dst.at[s, pl.ds(0, FF)], sem.at[s])

    def swap_w(src, dst, ss, rs, s):
        return remote(src.at[0, :, cols(s)], dst.at[s, pl.ds(FF, FF)], ss.at[s], rs.at[s], core)

    def start_local(s, _):
        load_tok(s, 0).start()
        load_tok(s, 1).start()
        load_w(wg_ref, wg, wgo, s).start()
        load_w(wd_ref, wd, wdo, s).start()
        return 0

    lax.fori_loop(0, NS, start_local, 0)
    wt[0] = wt_ref[...]

    bar = pltpu.get_barrier_semaphore()
    partners = [core]
    for dx in range(2):
        for dy in range(4):
            if (dx, dy) != (0, 0):
                partners.append(rel(dx, dy))
    for dz in range(8):
        if dz:
            partners.append(zdev(dz, lo))
        partners.append(zdev(dz, ol))
    for p in partners:
        pl.semaphore_signal(bar, inc=1, device_id=p, device_id_type=MESH)
    pre[...] = jnp.zeros_like(pre)
    pl.semaphore_wait(bar, len(partners))

    zpar = z % 2

    def item(j):
        return jnp.where(j < ZP, 2 * j + zpar, j + ZP)

    def other(j):
        return 2 * j + 1 - zpar

    def d1(j, d):
        s = item(j)
        return remote(
            xp.at[s, :, 0, 0], xp.at[s, :, 0, 3 if d == 0 else 1],
            s1s.at[j, d], s1r.at[j, d], yp if d == 0 else ym,
        )

    def d2(j, d):
        s = item(j)
        return remote(
            xp.at[s, d, 0, 3 if d == 0 else 1], xp.at[s, d, 0, 2],
            s2s.at[j, d], s2r.at[j, d], yp if d == 0 else ym,
        )

    def d3(j):
        s = item(j)
        return remote(xp.at[s, lo, 0], xp.at[s, lo, 1], s3s.at[j], s3r.at[j], outer)

    def d4(j):
        s = item(j)
        return remote(xp.at[s, ol, 1], xp.at[s, ol, 1], s4s.at[j], s4r.at[j], inner)

    def d5(j, d):
        s = item(j)
        step = jnp.where(j % 2 == 0, 1 - 2 * zpar, 2 * zpar - 1)
        to = dev(hi, y, k, (z + step + 8) % 8, lo)
        if d == 0:
            return remote(xp.at[s, :, 1], xp.at[s, :, 1], s5s.at[j, d], s5r.at[j, d], to)
        mid = xp.at[s, :, 0, pl.ds(1, 3)]
        return remote(mid, mid, s5s.at[j, d], s5r.at[j, d], to)

    def gate(s):
        load_w(wg_ref, wg, wgo, s).wait()
        swap_w(wg_ref, wg, wgs, wgr, s).wait_recv()

        @pl.loop(0, 4)
        def _(i):
            rows = pl.ds(pl.multiple_of(i * 256, 256), 256)
            acc = pre[rows, :]
            for h in range(2):
                xs = xp[s, h, i // 2, pl.ds((i % 2) * 2, 2)].reshape(256, HW)
                ws = wg[s, :, h * HW:(h + 1) * HW]
                acc = acc + lax.dot_general(
                    xs, ws, (((1,), (1,)), ((), ())), preferred_element_type=F32
                )
            pre[rows, :] = acc

    def send_wt():
        for dx in range(2):
            for dy in range(4):
                if (dx, dy) != (0, 0):
                    remote(wt_ref, wt.at[dx * 4 + (4 - dy) % 4], wts, wtr, rel(dx, dy)).start()

    def wait_wt():
        both = wt.at[pl.ds(1, 7)]
        cp = remote(both, both, wts, wtr, core)
        cp.wait_send()
        cp.wait_recv()

    def g_tick(t, _):
        @pl.when(t < NI)
        def _():
            s = item(t)
            load_tok(s, 0).wait()
            load_tok(s, 1).wait()
            d1(t, 0).start()
            d1(t, 1).start()

        @pl.when(t == 0)
        def _():
            send_wt()

        @pl.when(t < NP)
        def _():
            swap_w(wg_ref, wg, wgs, wgr, 2 * t).start()
            swap_w(wg_ref, wg, wgs, wgr, 2 * t + 1).start()

        @pl.when(t >= NP)
        def _():
            @pl.when(t < 2 * NP)
            def _():
                swap_w(wd_ref, wd, wds, wdr, 2 * (t - NP)).start()
                swap_w(wd_ref, wd, wds, wdr, 2 * (t - NP) + 1).start()

        @pl.when(jnp.logical_and(t >= 1, t - 1 < NI))
        def _():
            j = t - 1
            d1(j, 0).wait_recv()
            d2(j, 0).start()
            d1(j, 1).wait_recv()
            d2(j, 1).start()

        @pl.when(jnp.logical_and(t >= 2, t - 2 < NI))
        def _():
            j = t - 2
            d2(j, 0).wait_recv()
            d2(j, 1).wait_recv()
            d3(j).start()

        @pl.when(jnp.logical_and(t >= 3, t - 3 < NI))
        def _():
            j = t - 3
            d3(j).wait_recv()
            d4(j).start()

        @pl.when(jnp.logical_and(t >= 4, t - 4 < NI))
        def _():
            j = t - 4
            d4(j).wait_recv()

            @pl.when(j < ZP)
            def _():
                d5(j, 0).start()
                d5(j, 1).start()

            gate(item(j))

        @pl.when(jnp.logical_and(t >= 9, t - 9 < ZP))
        def _():
            j = t - 9
            s = other(j)
            load_tok(s, 0).wait()
            load_tok(s, 1).wait()
            d5(j, 0).wait_recv()
            d5(j, 1).wait_recv()
            gate(s)

        return 0

    lax.fori_loop(0, 13, g_tick, 0)

    def g_drain(j, _):
        for d in range(2):
            d1(j, d).wait_send()
            d2(j, d).wait_send()
        d3(j).wait_send()
        d4(j).wait_send()

        @pl.when(j < ZP)
        def _():
            d5(j, 0).wait_send()
            d5(j, 1).wait_send()

        return 0

    wait_wt()
    own = 2 * (e // 2) + k
    col = lax.broadcasted_iota(jnp.int32, (EXPERTS, FF2), 1)
    row = lax.broadcasted_iota(jnp.int32, (EXPERTS, FF2), 0)
    named = jnp.where(col < FF, own, own + 1 - 2 * k)
    sel = jnp.where(row == named, 1.0, 0.0).astype(F32)

    @pl.loop(0, 8)
    def _(b):
        rows = pl.ds(pl.multiple_of(b * ROWS, ROWS), ROWS)
        v = pre[rows, :]
        scale = lax.dot_general(
            wt[b], sel, (((0,), (0,)), ((), ())),
            preferred_element_type=F32, precision=lax.Precision.HIGHEST,
        )
        hid[rows, :] = (scale * (v / (1.0 + jnp.exp(-v)))).astype(BF)

    lax.fori_loop(0, NI, g_drain, 0)

    def down(s):
        load_w(wd_ref, wd, wdo, s).wait()
        swap_w(wd_ref, wd, wds, wdr, s).wait_recv()

        @pl.loop(0, 4)
        def _(i):
            rows = pl.ds(pl.multiple_of(i * 256, 256), 256)
            r = jnp.dot(hid[rows, :], wd[s], preferred_element_type=F32).astype(BF)
            for h in range(2):
                xp[s, h, i // 2, pl.ds((i % 2) * 2, 2)] = r[:, h * HW:(h + 1) * HW].reshape(2, ROWS, HW)

    def total(*parts):
        acc = parts[0].astype(F32)
        for part in parts[1:]:
            acc = acc + part.astype(F32)
        return acc

    top, low = pl.ds(0, 64), pl.ds(64, 64)

    def a1(p, d):
        return remote(xp.at[2 * p, d, :, 2], ry1.at[p, d], y1s.at[p, d], y1r.at[p, d], yp if d == 0 else ym)

    def a2(p, d):
        return remote(
            xp.at[2 * p, :, :, 1 if d == 0 else 3], ry2.at[p, d],
            y2s.at[p, d], y2r.at[p, d], yp if d == 0 else ym,
        )

    def a3(p, d):
        return remote(
            xp.at[2 * p, lo, 1, 0, top if d == 0 else low], rx1.at[p, d],
            x1s.at[p, d], x1r.at[p, d], inner if d == 0 else outer,
        )

    def a4(p, d):
        return remote(
            xp.at[2 * p, ol, d, 0], rx2.at[p, d],
            x2s.at[p, d], x2r.at[p, d], inner if d == 0 else outer,
        )

    def b1(p, d):
        return remote(
            xp.at[2 * p + 1, lo, 1, :, top if d == 0 else low], qx1.at[p, d],
            u1s.at[p, d], u1r.at[p, d], inner if d == 0 else outer,
        )

    def b2(p, d):
        return remote(
            xp.at[2 * p + 1, ol, d], qx2.at[p, d],
            u2s.at[p, d], u2r.at[p, d], inner if d == 0 else outer,
        )

    def b3(p, d):
        return remote(
            xp.at[2 * p + 1, lo, 0, 2, top if d == 0 else low], qy1.at[p, d],
            v1s.at[p, d], v1r.at[p, d], yp if d == 0 else ym,
        )

    def b4(p, d):
        return remote(
            xp.at[2 * p + 1, lo, 0, 1 if d == 0 else 3], qy2.at[p, d],
            v2s.at[p, d], v2r.at[p, d], yp if d == 0 else ym,
        )

    def z1(s):
        for dz in range(1, 8):
            remote(
                tz.at[s, (z + dz) % 8], tz.at[s, 8 + (7 - dz)], z1s.at[s], z1r.at[s], zdev(dz, lo)
            ).start()

    def z1_done(s):
        got = tz.at[s, pl.ds(8, 7)]
        return remote(got, got, z1s.at[s], z1r.at[s], core)

    def place(s):
        return o_ref.at[
            pl.ds(pl.multiple_of(z * 16, 16), 16),
            pl.ds(pl.multiple_of(s * CW + lo * HW, HW), HW),
        ]

    def keep(s):
        return pltpu.make_async_copy(fz.at[s], place(s), aglo.at[s])

    def z2(s):
        keep(s).start()
        for dz in range(8):
            if dz:
                remote(fz.at[s], place(s), ags.at[s], agr.at[s], zdev(dz, lo)).start()
            remote(fz.at[s], place(s), ags.at[s], agr.at[s], zdev(dz, ol)).start()

    def z2_done(s):
        return remote(tz.at[s], tz.at[s], ags.at[s], agr.at[s], core)

    def both(fn, p, what):
        for d in range(2):
            cp = fn(p, d)
            getattr(cp, what)()

    def at_stage(t, n):
        return jnp.logical_and(t >= n, t - n < NP)

    def s_tick(t, _):
        @pl.when(t < NP)
        def _():
            down(2 * t)
            both(a1, t, "start")
            down(2 * t + 1)
            both(b1, t, "start")

        @pl.when(at_stage(t, 1))
        def _():
            p = t - 1
            s = 2 * p
            both(a1, p, "wait_recv")
            xp[s, 0, :, 1] = total(xp[s, 0, :, 1], ry1[p, 0]).astype(BF)
            a2(p, 0).start()
            xp[s, 1, :, 3] = total(xp[s, 1, :, 3], ry1[p, 1]).astype(BF)
            a2(p, 1).start()
            s = 2 * p + 1
            both(b1, p, "wait_recv")
            xp[s, ol, 1, :, 0:64] = total(xp[s, ol, 1, :, 0:64], qx1[p, 0]).astype(BF)
            b2(p, 1).start()
            xp[s, ol, 0, :, 64:128] = total(xp[s, ol, 0, :, 64:128], qx1[p, 1]).astype(BF)
            b2(p, 0).start()

        @pl.when(at_stage(t, 2))
        def _():
            p = t - 2
            s = 2 * p
            both(a2, p, "wait_recv")
            for h in range(2):
                xp[s, h, :, 0] = total(xp[s, h, :, 0], ry2[p, 0, h], ry2[p, 1, h]).astype(BF)
            both(a3, p, "start")
            s = 2 * p + 1
            both(b2, p, "wait_recv")
            xp[s, lo, 0] = total(xp[s, lo, 0], qx2[p, 0], qx2[p, 1]).astype(BF)
            both(b3, p, "start")

        @pl.when(at_stage(t, 3))
        def _():
            p = t - 3
            s = 2 * p
            both(a3, p, "wait_recv")
            xp[s, ol, 1, 0, 0:64] = total(xp[s, ol, 1, 0, 0:64], rx1[p, 0]).astype(BF)
            a4(p, 1).start()
            xp[s, ol, 0, 0, 64:128] = total(xp[s, ol, 0, 0, 64:128], rx1[p, 1]).astype(BF)
            a4(p, 0).start()
            s = 2 * p + 1
            both(b3, p, "wait_recv")
            xp[s, lo, 0, 1, 0:64] = total(xp[s, lo, 0, 1, 0:64], qy1[p, 0]).astype(BF)
            b4(p, 0).start()
            xp[s, lo, 0, 3, 64:128] = total(xp[s, lo, 0, 3, 64:128], qy1[p, 1]).astype(BF)
            b4(p, 1).start()

        @pl.when(at_stage(t, 4))
        def _():
            p = t - 4
            s = 2 * p
            both(a4, p, "wait_recv")
            tz[s, 0:8] = total(xp[s, lo, 0, 0], rx2[p, 0], rx2[p, 1]).astype(BF).reshape(8, 16, HW)
            z1(s)
            s = 2 * p + 1
            both(b4, p, "wait_recv")
            tz[s, 0:8] = total(xp[s, lo, 0, 0], qy2[p, 0], qy2[p, 1]).astype(BF).reshape(8, 16, HW)
            z1(s)

        @pl.when(at_stage(t, 5))
        def _():
            p = t - 5
            for q in range(2):
                s = 2 * p + q
                z1_done(s).wait_recv()
                acc = tz[s, z].astype(F32)
                for i in range(7):
                    acc = acc + tz[s, 8 + i].astype(F32)
                fz[s] = acc.astype(BF)
                z2(s)

        return 0

    lax.fori_loop(0, NP + 5, s_tick, 0)

    def s_drain(p, _):
        for fn in (a1, a2, a3, a4, b1, b2, b3, b4):
            both(fn, p, "wait_send")
        for q in range(2):
            s = 2 * p + q
            swap_w(wg_ref, wg, wgs, wgr, s).wait_send()
            swap_w(wd_ref, wd, wds, wdr, s).wait_send()
            z1_done(s).wait_send()
            keep(s).wait()
            z2_done(s).wait_send()
            z2_done(s).wait_recv()
        return 0

    lax.fori_loop(0, NP, s_drain, 0)


def on_device(tokens, routes, route_weights, w_gate, w_down):
    ids = jnp.arange(EXPERTS, dtype=jnp.int32)[:, None, None]
    wt = jnp.sum(jnp.where(routes.T[None] == ids, route_weights.T[None], 0.0), 1)
    dma = pltpu.SemaphoreType.DMA
    sems = (
        [dma((NS, 2))] + [dma((NS,))] * 6 + [dma, dma]
        + [dma((NI, 2))] * 4 + [dma((NI,))] * 4 + [dma((ZP, 2))] * 2
        + [dma((NP, 2))] * 16 + [dma((NS,))] * 5
    )
    return pl.pallas_call(
        kernel,
        out_shape=jax.ShapeDtypeStruct((ROWS, D), BF),
        in_specs=[pl.BlockSpec(memory_space=pltpu.VMEM)] + [pl.BlockSpec(memory_space=pl.ANY)] * 3,
        out_specs=pl.BlockSpec(memory_space=pl.ANY),
        scratch_shapes=[
            pltpu.VMEM((NS, 2, 2, 4, ROWS, HW), BF),
            pltpu.VMEM((NS, FF2, CW), BF),
            pltpu.VMEM((NS, FF2, CW), BF),
            pltpu.VMEM((8 * ROWS, FF2), F32),
            pltpu.VMEM((8 * ROWS, FF2), BF),
            pltpu.VMEM((8, EXPERTS, ROWS), F32),
            pltpu.VMEM((NP, 2, 2, ROWS, HW), BF),
            pltpu.VMEM((NP, 2, 2, 2, ROWS, HW), BF),
            pltpu.VMEM((NP, 2, 64, HW), BF),
            pltpu.VMEM((NP, 2, ROWS, HW), BF),
            pltpu.VMEM((NP, 2, 4, 64, HW), BF),
            pltpu.VMEM((NP, 2, 4, ROWS, HW), BF),
            pltpu.VMEM((NP, 2, 64, HW), BF),
            pltpu.VMEM((NP, 2, ROWS, HW), BF),
            pltpu.VMEM((NS, 15, 16, HW), BF),
            pltpu.VMEM((NS, 16, HW), BF),
        ] + sems,
        compiler_params=pltpu.CompilerParams(
            collective_id=0, has_side_effects=True, vmem_limit_bytes=56 << 20
        ),
        cost_estimate=pl.CostEstimate(
            flops=4 * 8 * ROWS * FF2 * D, bytes_accessed=4 * FF * D * 2, transcendentals=8 * ROWS * FF2
        ),
        name="moe",
    )(wt, tokens, w_gate, w_down)


def solution(mesh):
    in_specs = (
        P("expert", None),
        P("expert", None),
        P("expert", None),
        P("expert", "cuts", None),
        P("expert", "cuts", None),
    )
    return jax.shard_map(
        on_device, mesh=mesh, in_specs=in_specs, out_specs=P("expert", None), check_vma=False
    )
```

```python
import jax
import jax.numpy as jnp
from jax import lax
from jax.experimental import pallas as pl
from jax.experimental.pallas import tpu as pltpu
from jax.sharding import PartitionSpec as P

MESH = pl.DeviceIdType.MESH
BF = jnp.bfloat16
F32 = jnp.float32

D = 6144
HALF = D // 2
FF = 336
FFP = 384
PAIR = 2 * FFP
ROWS = 128
EXPERTS = 16
NS = 6
CW = HALF // NS
HW = CW // 2
NJ = 2 * NS
RSLOT = {0: 0, 1: 1, 3: 2, 2: 3}


def kernel(
    wt_ref, tok_ref, wg_ref, wd_ref, o_ref,
    xp, pb, wg, wd, pre, es, er, hid, wt,
    ry1, ry2, rx1, rx2, tz, fz,
    tok_sem,
    wgo, wgs, wgr, wgzs, wgzr, wgls, wglr,
    wdo, wds, wdr, wdzs, wdzr, wdls, wdlr,
    wts, wtr,
    s1s, s1r, s2s, s2r, os_, or_, is_, ir_, exs, exr,
    y1s, y1r, y2s, y2r, x1s, x1r, x2s, x2r,
    z1s, z1r, ags, agr, aglo,
):
    e = lax.axis_index("expert")
    c = lax.axis_index("cuts")
    hi, y, k = e // 8, (e // 2) % 4, e % 2
    z, lo = c // 2, c % 2
    ol = 1 - lo
    zpar, zi = z % 2, z // 2

    def dev(hi_, y_, k_, z_, lo_):
        return (hi_ * 8 + y_ * 2 + k_, z_ * 2 + lo_)

    yp = dev(hi, (y + 1) % 4, k, z, lo)
    ym = dev(hi, (y + 3) % 4, k, z, lo)
    inner = dev(hi, y, k, z, ol)
    outer = dev(1 - hi, y, k, z, ol)
    core = dev(hi, y, 1 - k, z, lo)

    def zdev(dz, lo_):
        return dev(hi, y, k, (z + dz + 8) % 8, lo_)

    def rel(dx, dy):
        if dx == 0:
            return dev(hi, (y + dy) % 4, k, z, lo)
        return dev(1 - hi, (y + dy) % 4, k, z, ol)

    def remote(src, dst, ss, rs, to):
        return pltpu.make_async_remote_copy(
            src_ref=src, dst_ref=dst, send_sem=ss, recv_sem=rs, device_id=to, device_id_type=MESH
        )

    def cols(par, s):
        return pl.ds(pl.multiple_of(par * HALF + s * CW, CW), CW)

    def load_tok(s, h):
        at = pl.multiple_of(zpar * HALF + s * CW + h * HW, HW)
        return pltpu.make_async_copy(tok_ref.at[:, pl.ds(at, HW)], xp.at[s, h, 0, 0], tok_sem.at[s, h])

    real = pl.ds(0, FF)
    own_q, far_q = 3 * k, 2 - k

    class Weights:
        def __init__(self, src, dst, so, ss, sr, zs, zr, ls, lr):
            self.src, self.dst = src, dst
            self.so, self.ss, self.sr, self.zs, self.zr, self.ls, self.lr = so, ss, sr, zs, zr, ls, lr

        def local(self, s):
            return pltpu.make_async_copy(
                self.src.at[0, :, cols(zpar, s)], self.dst.at[s, own_q, real], self.so.at[s]
            )

        def swap(self, s):
            return remote(
                self.src.at[0, :, cols(zpar, s)], self.dst.at[s, own_q, real], self.ss.at[s], self.sr.at[s], core
            )

        def along(self, s):
            return remote(
                self.src.at[0, :, cols(1 - zpar, s)], self.dst.at[s, far_q, real],
                self.zs.at[s], self.zr.at[s], zdev(1 - 2 * k, lo),
            )

        def relay(self, s):
            ref = self.dst.at[s, far_q, real]
            return remote(ref, ref, self.ls.at[s], self.lr.at[s], core)

        def ready(self, s):
            self.local(s).wait()
            self.swap(s).wait_recv()
            self.relay(s).wait_recv()

        def drain(self, s):
            self.swap(s).wait_send()
            self.along(s).wait_send()
            self.relay(s).wait_send()

    gw = Weights(wg_ref, wg, wgo, wgs, wgr, wgzs, wgzr, wgls, wglr)
    dw = Weights(wd_ref, wd, wdo, wds, wdr, wdzs, wdzr, wdls, wdlr)

    def loop(n, body):
        def step(i, _):
            body(i)
            return 0

        lax.fori_loop(0, n, step, 0)

    def start_tok(s):
        load_tok(s, 0).start()
        load_tok(s, 1).start()

    def start_local(s):
        gw.local(s).start()
        dw.local(s).start()

    loop(NS, start_tok)

    bar = pltpu.get_barrier_semaphore()
    partners = [core]
    for dx in range(2):
        for dy in range(4):
            if (dx, dy) != (0, 0):
                partners.append(rel(dx, dy))
    for dz in range(8):
        if dz:
            partners.append(zdev(dz, lo))
        partners.append(zdev(dz, ol))
    for p in partners:
        pl.semaphore_signal(bar, inc=1, device_id=p, device_id_type=MESH)
    loop(NS, start_local)
    wt[0] = wt_ref[...]

    def clear_pad(s):
        for q in range(4):
            wg[s, q, FF:FFP, :] = jnp.zeros((FFP - FF, CW), BF)
            wd[s, q, FF:FFP, :] = jnp.zeros((FFP - FF, CW), BF)

    loop(NS, clear_pad)
    pl.semaphore_wait(bar, len(partners))

    def s1(j, d):
        return remote(
            xp.at[j, :, 0, 0], xp.at[j, :, 0, 2 - d], s1s.at[j, d], s1r.at[j, d], yp if d == 0 else ym
        )

    def s2(j, d):
        return remote(
            xp.at[j, d, 0, 2 - d], xp.at[j, d, 0, 3], s2s.at[j, d], s2r.at[j, d], yp if d == 0 else ym
        )

    part = (pl.ds(0, 1), pl.ds(1, 2), pl.ds(3, 1))

    def og(j, n):
        return remote(xp.at[j, lo, 0, part[n]], xp.at[j, lo, 1, part[n]], os_.at[j, n], or_.at[j, n], outer)

    def ig(j, n):
        ref = xp.at[j, ol, 1, part[n]]
        return remote(ref, ref, is_.at[j, n], ir_.at[j, n], inner)

    def gate(j, dx, r0, nr):
        m = nr * ROWS
        row0 = (dx * 4 + r0) * ROWS

        @pl.loop(0, 2)
        def _(i):
            acc = pre[i, row0:row0 + m, :]
            for h in range(2):
                xs = xp[j, h, dx, r0:r0 + nr].reshape(m, HW)
                ws = wg[j, pl.ds(2 * i, 2), :, h * HW:(h + 1) * HW].reshape(PAIR, HW)
                acc = acc + lax.dot_general(xs, ws, (((1,), (1,)), ((), ())), preferred_element_type=F32)
            pre[i, row0:row0 + m, :] = acc

    def ex(n, d):
        rows = (pl.ds(0, 384), pl.ds(384, 128), pl.ds(512, 512))[n]
        return remote(es.at[d, rows], er.at[d, rows], exs.at[n, d], exr.at[n, d], zdev(1 - 2 * d, lo))

    def exchange(n):
        b0, nb = ((0, 3), (3, 1), (4, 4))[n]

        def stage(b):
            rows = pl.ds(pl.multiple_of((b0 + b) * ROWS, ROWS), ROWS)
            for d in range(2):
                es[d, rows, :] = pre[d, rows, :].astype(BF)

        loop(nb, stage)
        ex(n, 0).start()
        ex(n, 1).start()

    def first(j):
        gw.along(j).start()
        gw.swap(j).start()

    loop(NS, first)

    def l0(j):
        load_tok(j, 0).wait()
        load_tok(j, 1).wait()
        s1(j, 0).start()
        s1(j, 1).start()
        og(j, 0).start()

    loop(NS, l0)
    for dx in range(2):
        for dy in range(4):
            if (dx, dy) != (0, 0):
                remote(wt_ref, wt.at[dx * 4 + RSLOT[(4 - dy) % 4]], wts, wtr, rel(dx, dy)).start()
    dw.along(0).start()

    def clear_pre(b):
        rows = pl.ds(pl.multiple_of(b * ROWS, ROWS), ROWS)
        for i in range(2):
            pre[i, rows, :] = jnp.zeros((ROWS, PAIR), F32)

    loop(8, clear_pre)

    def l1(t):
        @pl.when(t < NS)
        def _():
            s1(t, 0).wait_recv()
            s2(t, 0).start()
            s1(t, 1).wait_recv()
            s2(t, 1).start()
            og(t, 1).start()
            og(t, 0).wait_recv()
            ig(t, 0).start()
            gw.along(t).wait_recv()
            gw.relay(t).start()

        @pl.when(jnp.logical_and(t >= 2, t < NS))
        def _():
            og(t - 2, 1).wait_recv()
            ig(t - 2, 1).start()

        @pl.when(t >= 1)
        def _():
            gw.ready(t - 1)
            gate(t - 1, 0, 0, 3)

    loop(NS + 1, l1)
    exchange(0)

    def l2(j):
        s2(j, 0).wait_recv()
        s2(j, 1).wait_recv()
        og(j, 2).start()

        @pl.when(j < 2)
        def _():
            og(j + 4, 1).wait_recv()
            ig(j + 4, 1).start()

        dw.swap(j).start()
        gate(j, 0, 3, 1)

    loop(NS, l2)
    exchange(1)
    dw.along(1).start()

    def l3(t):
        @pl.when(t < NS)
        def _():
            og(t, 2).wait_recv()
            ig(t, 2).start()

        @pl.when(t >= 2)
        def _():
            for n in range(3):
                ig(t - 2, n).wait_recv()
            gate(t - 2, 1, 0, 4)

    loop(NS + 2, l3)
    exchange(2)

    def more(s):
        dw.along(s + 2).start()

    loop(NS - 2, more)

    def relay_down(s):
        dw.along(s).wait_recv()
        dw.relay(s).start()

    relay_down(0)

    got = wt.at[pl.ds(1, 7)]
    all_wt = remote(got, got, wts, wtr, core)
    all_wt.wait_send()
    all_wt.wait_recv()
    col = lax.broadcasted_iota(jnp.int32, (EXPERTS, PAIR), 1)
    row = lax.broadcasted_iota(jnp.int32, (EXPERTS, PAIR), 0)
    e0 = 2 * (e // 2)
    hit0 = jnp.logical_and(row == e0, col < FF)
    hit1 = jnp.logical_and(row == e0 + 1, jnp.logical_and(col >= FFP, col < FFP + FF))
    sel = jnp.where(jnp.logical_or(hit0, hit1), 1.0, 0.0).astype(F32)

    def hidden(b):
        rows = pl.ds(pl.multiple_of(b * ROWS, ROWS), ROWS)
        scale = lax.dot_general(
            wt[b], sel, (((0,), (0,)), ((), ())),
            preferred_element_type=F32, precision=lax.Precision.HIGHEST,
        )
        for i in range(2):
            v = pre[i, rows, :] + er[1 - i, rows, :].astype(F32)
            hid[rows, i * PAIR:(i + 1) * PAIR] = (scale * (v / (1.0 + jnp.exp(-v)))).astype(BF)

    for n in range(2):
        ex(n, 0).wait_recv()
        ex(n, 1).wait_recv()
    loop(4, hidden)
    relay_down(1)

    def down(s, dx):
        @pl.loop(0, 2)
        def _(i):
            rows = pl.ds(pl.multiple_of(dx * 512 + i * 256, 256), 256)
            r = jnp.dot(hid[rows, :], wd[s].reshape(4 * FFP, CW), preferred_element_type=F32).astype(BF)
            for h in range(2):
                pb[s, h, dx, pl.ds(i * 2, 2)] = r[:, h * HW:(h + 1) * HW].reshape(2, ROWS, HW)

    def total(*parts):
        acc = parts[0].astype(F32)
        for p in parts[1:]:
            acc = acc + p.astype(F32)
        return acc.astype(BF)

    top, low = pl.ds(0, 64), pl.ds(64, 64)

    def a1(s, dx, d):
        return remote(pb.at[s, d, dx, 3], ry1.at[s, dx, d], y1s.at[s, dx, d], y1r.at[s, dx, d], yp if d == 0 else ym)

    def a2(s, dx, d):
        return remote(
            pb.at[s, :, dx, 1 + d], ry2.at[s, dx, d], y2s.at[s, dx, d], y2r.at[s, dx, d], yp if d == 0 else ym
        )

    def a3(s, d):
        return remote(
            pb.at[s, lo, 1, 0, top if d == 0 else low], rx1.at[s, d],
            x1s.at[s, d], x1r.at[s, d], inner if d == 0 else outer,
        )

    def a4(s, d):
        return remote(
            pb.at[s, ol, d, 0], rx2.at[s, d], x2s.at[s, d], x2r.at[s, d], inner if d == 0 else outer
        )

    def z1(s):
        for dz in range(1, 4):
            remote(
                tz.at[s, (zi + dz) % 4], tz.at[s, 4 + (3 - dz)], z1s.at[s], z1r.at[s], zdev(2 * dz, lo)
            ).start()

    def z1_done(s):
        ref = tz.at[s, pl.ds(4, 3)]
        return remote(ref, ref, z1s.at[s], z1r.at[s], core)

    def place(s):
        return o_ref.at[
            pl.ds(pl.multiple_of(zi * 32, 32), 32),
            pl.ds(pl.multiple_of(zpar * HALF + s * CW + lo * HW, HW), HW),
        ]

    def keep(s):
        return pltpu.make_async_copy(fz.at[s], place(s), aglo.at[s])

    def z2(s):
        keep(s).start()
        for dz in range(8):
            if dz:
                remote(fz.at[s], place(s), ags.at[s], agr.at[s], zdev(dz, lo)).start()
            remote(fz.at[s], place(s), ags.at[s], agr.at[s], zdev(dz, ol)).start()

    def z2_done(s):
        return remote(tz.at[s], tz.at[s], ags.at[s], agr.at[s], core)

    def job(t):
        early = t < 4
        return jnp.where(early, t % 2, t // 2), jnp.where(early, t // 2, t % 2)

    def r_tick(t):
        @pl.when(t == 2)
        def _():
            ex(2, 0).wait_recv()
            ex(2, 1).wait_recv()

            def late(b):
                hidden(b + 4)

            loop(4, late)

        @pl.when(t < NJ)
        def _():
            s, dx = job(t)

            @pl.when(dx == 0)
            def _():
                dw.ready(s)

            down(s, dx)
            a1(s, dx, 0).start()
            a1(s, dx, 1).start()

        @pl.when(jnp.logical_and(t >= 1, t - 1 < NJ))
        def _():
            s, dx = job(t - 1)
            for d in range(2):
                a1(s, dx, d).wait_recv()
                pb[s, d, dx, 1 + d] = total(pb[s, d, dx, 1 + d], ry1[s, dx, d])
                a2(s, dx, d).start()

        @pl.when(jnp.logical_and(t >= 2, t - 2 < NJ))
        def _():
            s, dx = job(t - 2)
            a2(s, dx, 0).wait_recv()
            a2(s, dx, 1).wait_recv()
            pb[s, :, dx, 0] = total(pb[s, :, dx, 0], ry2[s, dx, 0], ry2[s, dx, 1])

        def stage(n, fn):
            @pl.when(jnp.logical_and(t % 2 == n % 2, jnp.logical_and(t >= n, t - n < NJ)))
            def _():
                fn((t - n) // 2)

        def go_x1(s):
            a3(s, 0).start()
            a3(s, 1).start()

        def go_x2(s):
            a3(s, 0).wait_recv()
            pb[s, ol, 1, 0, 0:64] = total(pb[s, ol, 1, 0, 0:64], rx1[s, 0])
            a4(s, 1).start()
            a3(s, 1).wait_recv()
            pb[s, ol, 0, 0, 64:128] = total(pb[s, ol, 0, 0, 64:128], rx1[s, 1])
            a4(s, 0).start()

        def go_z1(s):
            a4(s, 0).wait_recv()
            a4(s, 1).wait_recv()
            tz[s, 0:4] = total(pb[s, lo, 0, 0], rx2[s, 0], rx2[s, 1]).reshape(4, 32, HW)
            z1(s)

        def go_z2(s):
            z1_done(s).wait_recv()
            fz[s] = total(tz[s, zi], tz[s, 4], tz[s, 5], tz[s, 6])
            z2(s)

        stage(4, go_x1)
        stage(5, go_x2)
        stage(6, go_z1)
        stage(7, go_z2)

        @pl.when(jnp.logical_and(t % 2 == 1, jnp.logical_and(t >= 3, t < NJ - 1)))
        def _():
            relay_down((t + 1) // 2)

    loop(NJ + 6, r_tick)

    def drain(s):
        gw.drain(s)
        dw.drain(s)
        for d in range(2):
            s1(s, d).wait_send()
            s2(s, d).wait_send()
            a3(s, d).wait_send()
            a4(s, d).wait_send()
            for dx in range(2):
                a1(s, dx, d).wait_send()
                a2(s, dx, d).wait_send()
        for n in range(3):
            og(s, n).wait_send()
            ig(s, n).wait_send()
        z1_done(s).wait_send()
        keep(s).wait()
        z2_done(s).wait_send()
        z2_done(s).wait_recv()

    loop(NS, drain)
    for n in range(3):
        ex(n, 0).wait_send()
        ex(n, 1).wait_send()


def on_device(tokens, routes, route_weights, w_gate, w_down):
    ids = jnp.arange(EXPERTS, dtype=jnp.int32)[:, None, None]
    wt = jnp.sum(jnp.where(routes.T[None] == ids, route_weights.T[None], 0.0), 1)
    dma = pltpu.SemaphoreType.DMA
    sems = (
        [dma((NS, 2))] + [dma((NS,))] * 14 + [dma, dma]
        + [dma((NS, 2))] * 4 + [dma((NS, 3))] * 4 + [dma((3, 2))] * 2
        + [dma((NS, 2, 2))] * 4 + [dma((NS, 2))] * 4 + [dma((NS,))] * 5
    )
    return pl.pallas_call(
        kernel,
        out_shape=jax.ShapeDtypeStruct((ROWS, D), BF),
        in_specs=[pl.BlockSpec(memory_space=pltpu.VMEM)] + [pl.BlockSpec(memory_space=pl.ANY)] * 3,
        out_specs=pl.BlockSpec(memory_space=pl.ANY),
        scratch_shapes=[
            pltpu.VMEM((NS, 2, 2, 4, ROWS, HW), BF),
            pltpu.VMEM((NS, 2, 2, 4, ROWS, HW), BF),
            pltpu.VMEM((NS, 4, FFP, CW), BF),
            pltpu.VMEM((NS, 4, FFP, CW), BF),
            pltpu.VMEM((2, 8 * ROWS, PAIR), F32),
            pltpu.VMEM((2, 8 * ROWS, PAIR), BF),
            pltpu.VMEM((2, 8 * ROWS, PAIR), BF),
            pltpu.VMEM((8 * ROWS, 2 * PAIR), BF),
            pltpu.VMEM((8, EXPERTS, ROWS), F32),
            pltpu.VMEM((NS, 2, 2, ROWS, HW), BF),
            pltpu.VMEM((NS, 2, 2, 2, ROWS, HW), BF),
            pltpu.VMEM((NS, 2, 64, HW), BF),
            pltpu.VMEM((NS, 2, ROWS, HW), BF),
            pltpu.VMEM((NS, 15, 32, HW), BF),
            pltpu.VMEM((NS, 32, HW), BF),
        ] + sems,
        compiler_params=pltpu.CompilerParams(
            collective_id=0, has_side_effects=True, vmem_limit_bytes=58 << 20
        ),
        cost_estimate=pl.CostEstimate(
            flops=8 * 8 * ROWS * FF * D, bytes_accessed=4 * FF * D * 2, transcendentals=32 * ROWS * FF
        ),
        name="moe",
    )(wt, tokens, w_gate, w_down)


def solution(mesh):
    in_specs = (
        P("expert", None),
        P("expert", None),
        P("expert", None),
        P("expert", "cuts", None),
        P("expert", "cuts", None),
    )
    return jax.shard_map(
        on_device, mesh=mesh, in_specs=in_specs, out_specs=P("expert", None), check_vma=False
    )
```

```python
import jax
import jax.numpy as jnp
from jax import lax
from jax.experimental import pallas as pl
from jax.experimental.pallas import tpu as pltpu
from jax.sharding import PartitionSpec as P

MESH = pl.DeviceIdType.MESH
BF = jnp.bfloat16
F32 = jnp.float32

D = 6144
HALF = D // 2
FF = 336
FFP = 384
PAIR = 2 * FFP
ROWS = 128
EXPERTS = 16
NS = 6
CW = HALF // NS
HW = CW // 2
NJ = 2 * NS
EARLY = 3
CAP = 64
RSLOT = {0: 0, 1: 1, 3: 2, 2: 3}


def kernel(
    wt_ref, tok_ref, wg_ref, wd_ref, o_ref,
    xp, pb, wg, wd, pre, es, er, hid, wt, pick,
    ry1, ry2, rx, tz, fz,
    tok_sem,
    wgo, wgs, wgr, wgzs, wgzr, wgls, wglr,
    wdo, wds, wdr, wdzs, wdzr, wdls, wdlr,
    wts, wtr,
    s1s, s1r, s2s, s2r, os_, or_, is_, ir_, exs, exr,
    y1s, y1r, y2s, y2r, xs_, xr_,
    z1s, z1r, ags, agr, aglo, ils, ilr,
):
    e = lax.axis_index("expert")
    c = lax.axis_index("cuts")
    hi, y, k = e // 8, (e // 2) % 4, e % 2
    z, lo = c // 2, c % 2
    ol = 1 - lo
    zpar, zi = z % 2, z // 2

    def dev(hi_, y_, k_, z_, lo_):
        return (hi_ * 8 + y_ * 2 + k_, z_ * 2 + lo_)

    yp = dev(hi, (y + 1) % 4, k, z, lo)
    ym = dev(hi, (y + 3) % 4, k, z, lo)
    inner = dev(hi, y, k, z, ol)
    outer = dev(1 - hi, y, k, z, ol)
    across = dev(1 - hi, y, k, z, lo)
    core = dev(hi, y, 1 - k, z, lo)

    def zdev(dz, lo_):
        return dev(hi, y, k, (z + dz + 8) % 8, lo_)

    def rel(dx, dy):
        if dx == 0:
            return dev(hi, (y + dy) % 4, k, z, lo)
        return dev(1 - hi, (y + dy) % 4, k, z, ol)

    def remote(src, dst, ss, rs, to):
        return pltpu.make_async_remote_copy(
            src_ref=src, dst_ref=dst, send_sem=ss, recv_sem=rs, device_id=to, device_id_type=MESH
        )

    def cols(par, s):
        return pl.ds(pl.multiple_of(par * HALF + s * CW, CW), CW)

    def load_tok(s, h):
        at = pl.multiple_of(zpar * HALF + s * CW + h * HW, HW)
        return pltpu.make_async_copy(tok_ref.at[:, pl.ds(at, HW)], xp.at[s, h, 0, 0], tok_sem.at[s, h])

    real = pl.ds(0, FF)
    own_q, far_q = 3 * k, 2 - k

    class Weights:
        def __init__(self, src, dst, so, ss, sr, zs, zr, ls, lr):
            self.src, self.dst = src, dst
            self.so, self.ss, self.sr, self.zs, self.zr, self.ls, self.lr = so, ss, sr, zs, zr, ls, lr

        def local(self, s):
            return pltpu.make_async_copy(
                self.src.at[0, :, cols(zpar, s)], self.dst.at[s, own_q, real], self.so.at[s]
            )

        def swap(self, s):
            return remote(
                self.src.at[0, :, cols(zpar, s)], self.dst.at[s, own_q, real], self.ss.at[s], self.sr.at[s], core
            )

        def along(self, s):
            return remote(
                self.src.at[0, :, cols(1 - zpar, s)], self.dst.at[s, far_q, real],
                self.zs.at[s], self.zr.at[s], zdev(1 - 2 * k, lo),
            )

        def relay(self, s):
            ref = self.dst.at[s, far_q, real]
            return remote(ref, ref, self.ls.at[s], self.lr.at[s], core)

        def ready(self, s):
            self.local(s).wait()
            self.swap(s).wait_recv()
            self.relay(s).wait_recv()

        def drain(self, s):
            self.swap(s).wait_send()
            self.along(s).wait_send()
            self.relay(s).wait_send()

    gw = Weights(wg_ref, wg, wgo, wgs, wgr, wgzs, wgzr, wgls, wglr)
    dw = Weights(wd_ref, wd, wdo, wds, wdr, wdzs, wdzr, wdls, wdlr)

    def loop(n, body):
        def step(i, _):
            body(i)
            return 0

        lax.fori_loop(0, n, step, 0)

    def start_tok(s):
        load_tok(s, 0).start()
        load_tok(s, 1).start()

    def start_local(s):
        gw.local(s).start()
        dw.local(s).start()

    loop(NS, start_tok)

    bar = pltpu.get_barrier_semaphore()
    partners = [core]
    for dx in range(2):
        for dy in range(4):
            if (dx, dy) != (0, 0):
                partners.append(rel(dx, dy))
    for dz in range(1, 8):
        partners.append(zdev(dz, lo))
        partners.append(zdev(dz, ol))
    partners += [inner, across]
    for p in partners:
        pl.semaphore_signal(bar, inc=1, device_id=p, device_id_type=MESH)
    loop(NS, start_local)
    wt[0] = wt_ref[...]

    def clear_pad(s):
        for q in range(4):
            wg[s, q, FF:FFP, :] = jnp.zeros((FFP - FF, CW), BF)
            wd[s, q, FF:FFP, :] = jnp.zeros((FFP - FF, CW), BF)

    loop(NS, clear_pad)
    pl.semaphore_wait(bar, len(partners))

    def s1(j, d):
        return remote(
            xp.at[j, :, 0, 0], xp.at[j, :, 0, 2 - d], s1s.at[j, d], s1r.at[j, d], yp if d == 0 else ym
        )

    def s2(j, d):
        return remote(
            xp.at[j, d, 0, 2 - d], xp.at[j, d, 0, 3], s2s.at[j, d], s2r.at[j, d], yp if d == 0 else ym
        )

    part = (pl.ds(0, 1), pl.ds(1, 2), pl.ds(3, 1))

    def og(j, n):
        return remote(xp.at[j, lo, 0, part[n]], xp.at[j, lo, 1, part[n]], os_.at[j, n], or_.at[j, n], outer)

    def ig(j, n):
        ref = xp.at[j, ol, 1, part[n]]
        return remote(ref, ref, is_.at[j, n], ir_.at[j, n], inner)

    def gate(j, dx, r0, nr):
        m = nr * ROWS
        row0 = (dx * 4 + r0) * ROWS

        @pl.loop(0, 2)
        def _(i):
            acc = pre[i, row0:row0 + m, :]
            for h in range(2):
                xs = xp[j, h, dx, r0:r0 + nr].reshape(m, HW)
                ws = wg[j, pl.ds(2 * i, 2), :, h * HW:(h + 1) * HW].reshape(PAIR, HW)
                acc = acc + lax.dot_general(xs, ws, (((1,), (1,)), ((), ())), preferred_element_type=F32)
            pre[i, row0:row0 + m, :] = acc

    def ex(n, d):
        blocks = pl.ds(4 * n, 4)
        return remote(es.at[d, blocks], er.at[d, blocks], exs.at[n, d], exr.at[n, d], zdev(1 - 2 * d, lo))

    def exchange(n):
        def stage(i):
            b = 4 * n + i
            rows = pl.ds(pl.multiple_of(b * ROWS, ROWS), ROWS)
            for d in range(2):
                for q in range(2):
                    v = pre[d, rows, q * FFP:(q + 1) * FFP].astype(BF)
                    es[d, b, :, q * FFP:(q + 1) * FFP] = jnp.dot(
                        pick[b, q], v, preferred_element_type=F32
                    ).astype(BF)

        loop(4, stage)
        ex(n, 0).start()
        ex(n, 1).start()

    e0 = 2 * (e // 2)

    def make_pick():
        got = wt.at[pl.ds(1, 7)]
        all_wt = remote(got, got, wts, wtr, core)
        all_wt.wait_send()
        all_wt.wait_recv()
        ri = lax.broadcasted_iota(jnp.int32, (ROWS, ROWS), 0)
        ci = lax.broadcasted_iota(jnp.int32, (ROWS, ROWS), 1)
        upto = jnp.where(ri <= ci, 1.0, 0.0).astype(BF)
        row = lax.broadcasted_iota(jnp.int32, (EXPERTS, ROWS), 0)
        slot = lax.broadcasted_iota(jnp.int32, (CAP, ROWS), 0).astype(F32)

        def block(b):
            hit = jnp.where(wt[b] > 0.0, 1.0, 0.0)
            place = jnp.dot(hit.astype(BF), upto, preferred_element_type=F32) * hit - 1.0
            for q in range(2):
                mine = jnp.sum(jnp.where(row == e0 + q, place, 0.0), axis=0, keepdims=True)
                pick[b, q] = jnp.where(slot == mine, 1.0, 0.0).astype(BF)

        loop(8, block)

    def send_own(j):
        load_tok(j, 0).wait()
        load_tok(j, 1).wait()
        s1(j, 0).start()
        s1(j, 1).start()
        og(j, 0).start()

    def swap_gate(j):
        gw.swap(j).start()

    for j in range(2):
        gw.along(j).start()
        send_own(j)
    loop(NS, swap_gate)
    for dx in range(2):
        for dy in range(4):
            if (dx, dy) != (0, 0):
                remote(wt_ref, wt.at[dx * 4 + RSLOT[(4 - dy) % 4]], wts, wtr, rel(dx, dy)).start()

    def clear_pre(b):
        rows = pl.ds(pl.multiple_of(b * ROWS, ROWS), ROWS)
        for i in range(2):
            pre[i, rows, :] = jnp.zeros((ROWS, PAIR), F32)

    loop(8, clear_pre)

    def at(t, lag):
        return jnp.logical_and(t >= lag, t < NS + lag)

    def g_tick(t):
        @pl.when(t < NS)
        def _():
            s1(t, 0).wait_recv()
            s2(t, 0).start()
            s1(t, 1).wait_recv()
            s2(t, 1).start()
            og(t, 1).start()

        @pl.when(t + 2 < NS)
        def _():
            send_own(t + 2)
            gw.along(t + 2).start()

        @pl.when(jnp.logical_and(t + 2 >= NS, t + 2 < NS + 4))
        def _():
            dw.along(t + 2 - NS).start()

        @pl.when(t < NS)
        def _():
            og(t, 0).wait_recv()
            ig(t, 0).start()
            dw.swap(t).start()

        @pl.when(at(t, 1))
        def _():
            s2(t - 1, 0).wait_recv()
            s2(t - 1, 1).wait_recv()
            og(t - 1, 2).start()

        @pl.when(at(t, 2))
        def _():
            og(t - 2, 1).wait_recv()
            ig(t - 2, 1).start()

        @pl.when(at(t, 3))
        def _():
            og(t - 3, 2).wait_recv()
            ig(t - 3, 2).start()

        @pl.when(t < NS)
        def _():
            gw.along(t).wait_recv()
            gw.relay(t).start()

        @pl.when(t == 2)
        def _():
            make_pick()

        @pl.when(at(t, 1))
        def _():
            gw.ready(t - 1)
            gate(t - 1, 0, 0, 4)

        @pl.when(t == NS)
        def _():
            exchange(0)

        @pl.when(at(t, 4))
        def _():
            for n in range(3):
                ig(t - 4, n).wait_recv()
            gate(t - 4, 1, 0, 4)

    loop(NS + 4, g_tick)
    exchange(1)

    def relay_down(s):
        dw.along(s).wait_recv()
        dw.relay(s).start()

    relay_down(0)

    col = lax.broadcasted_iota(jnp.int32, (EXPERTS, PAIR), 1)
    row = lax.broadcasted_iota(jnp.int32, (EXPERTS, PAIR), 0)
    hit0 = jnp.logical_and(row == e0, col < FF)
    hit1 = jnp.logical_and(row == e0 + 1, jnp.logical_and(col >= FFP, col < FFP + FF))
    sel = jnp.where(jnp.logical_or(hit0, hit1), 1.0, 0.0).astype(F32)

    def hidden(b):
        rows = pl.ds(pl.multiple_of(b * ROWS, ROWS), ROWS)
        scale = lax.dot_general(
            wt[b], sel, (((0,), (0,)), ((), ())),
            preferred_element_type=F32, precision=lax.Precision.HIGHEST,
        )
        for i in range(2):
            for q in range(2):
                at = slice(q * FFP, (q + 1) * FFP)
                more = lax.dot_general(
                    pick[b, q], er[1 - i, b, :, at], (((0,), (0,)), ((), ())), preferred_element_type=F32
                )
                v = pre[i, rows, at] + more
                to = i * PAIR + q * FFP
                hid[rows, to:to + FFP] = (scale[:, at] * (v / (1.0 + jnp.exp(-v)))).astype(BF)

    ex(0, 0).wait_recv()
    ex(0, 1).wait_recv()
    loop(4, hidden)
    relay_down(1)

    def down(s, dx):
        @pl.loop(0, 2)
        def _(i):
            rows = pl.ds(pl.multiple_of(dx * 512 + i * 256, 256), 256)
            r = jnp.dot(hid[rows, :], wd[s].reshape(4 * FFP, CW), preferred_element_type=F32).astype(BF)
            for h in range(2):
                pb[s, h, dx, pl.ds(i * 2, 2)] = r[:, h * HW:(h + 1) * HW].reshape(2, ROWS, HW)

    def total(*parts):
        acc = parts[0].astype(F32)
        for p in parts[1:]:
            acc = acc + p.astype(F32)
        return acc.astype(BF)

    def a1(s, dx, d):
        return remote(pb.at[s, d, dx, 3], ry1.at[s, dx, d], y1s.at[s, dx, d], y1r.at[s, dx, d], yp if d == 0 else ym)

    def a2(s, dx, d):
        return remote(
            pb.at[s, :, dx, 1 + d], ry2.at[s, dx, d], y2s.at[s, dx, d], y2r.at[s, dx, d], yp if d == 0 else ym
        )

    def a3(s, n):
        src = pb.at[s, ol, n, 0] if n < 2 else pb.at[s, lo, 1, 0]
        return remote(src, rx.at[s, n], xs_.at[s, n], xr_.at[s, n], (inner, outer, across)[n])

    def z1(s):
        for dz in range(1, 4):
            remote(
                tz.at[s, (zi + dz) % 4], tz.at[s, 4 + (3 - dz)], z1s.at[s], z1r.at[s], zdev(2 * dz, lo)
            ).start()

    def z1_done(s):
        ref = tz.at[s, pl.ds(4, 3)]
        return remote(ref, ref, z1s.at[s], z1r.at[s], core)

    def place(s):
        return o_ref.at[
            pl.ds(pl.multiple_of(zi * 32, 32), 32),
            pl.ds(pl.multiple_of(zpar * HALF + s * CW + lo * HW, HW), HW),
        ]

    def keep(s):
        return pltpu.make_async_copy(fz.at[s], place(s), aglo.at[s])

    def z2(s):
        keep(s).start()
        for dz in range(1, 8):
            remote(fz.at[s], place(s), ags.at[s], agr.at[s], zdev(dz, lo)).start()

        @pl.when(s == NS - 1)
        def _():
            for dz in range(8):
                remote(fz.at[s], place(s), ils.at[s, dz % 2], ilr.at[s, zpar], zdev(dz, ol)).start()

    def z2_done(s):
        return remote(tz.at[s], tz.at[s], ags.at[s], agr.at[s], core)

    def cross(s, par):
        at = pl.multiple_of(par * HALF + s * CW + lo * HW, HW)
        ref = o_ref.at[:, pl.ds(at, HW)]
        return remote(ref, ref, ils.at[s, par], ilr.at[s, par], inner)

    def job(t):
        early = t < 2 * EARLY
        return jnp.where(early, t % EARLY, t // 2), jnp.where(early, t // EARLY, t % 2)

    def r_tick(t):
        @pl.when(t == EARLY)
        def _():
            ex(1, 0).wait_recv()
            ex(1, 1).wait_recv()
            dw.along(4).start()

            def late(b):
                hidden(b + 4)

            loop(4, late)

        @pl.when(t == EARLY + 1)
        def _():
            dw.along(5).start()

        @pl.when(t < NJ)
        def _():
            s, dx = job(t)

            @pl.when(dx == 0)
            def _():
                dw.ready(s)

            down(s, dx)
            a1(s, dx, 0).start()
            a1(s, dx, 1).start()

        @pl.when(jnp.logical_and(t >= 1, t - 1 < NJ))
        def _():
            s, dx = job(t - 1)
            for d in range(2):
                a1(s, dx, d).wait_recv()
                pb[s, d, dx, 1 + d] = total(pb[s, d, dx, 1 + d], ry1[s, dx, d])
                a2(s, dx, d).start()

        @pl.when(jnp.logical_and(t >= 3, t - 3 < NJ))
        def _():
            s, dx = job(t - 3)
            a2(s, dx, 0).wait_recv()
            a2(s, dx, 1).wait_recv()
            pb[s, :, dx, 0] = total(pb[s, :, dx, 0], ry2[s, dx, 0], ry2[s, dx, 1])

        def stage(n, fn):
            u = t - EARLY - n
            near = jnp.logical_and(u >= 0, u < EARLY)
            s = jnp.where(near, u, (u + EARLY - 1) // 2)
            far = jnp.logical_and((u + EARLY - 1) % 2 == 0, jnp.logical_and(u > EARLY, s < NS))

            @pl.when(jnp.logical_or(near, far))
            def _():
                fn(s)

        def go_x(s):
            for n in range(3):
                a3(s, n).start()

        def go_z1(s):
            for n in range(3):
                a3(s, n).wait_recv()
            tz[s, 0:4] = total(pb[s, lo, 0, 0], rx[s, 0], rx[s, 1], rx[s, 2]).reshape(4, 32, HW)
            z1(s)

        def go_z2(s):
            z1_done(s).wait_recv()
            fz[s] = total(tz[s, zi], tz[s, 4], tz[s, 5], tz[s, 6])
            z2(s)

        def go_cross(s):
            keep(s).wait()
            z2_done(s).wait_recv()

            @pl.when(s < NS - 1)
            def _():
                cross(s, 0).start()
                cross(s, 1).start()

        stage(3, go_x)
        stage(5, go_z1)
        stage(7, go_z2)
        stage(9, go_cross)

        ahead = t + 2 < EARLY
        late_s = t // 2 + 1
        follow = jnp.logical_and(t % 2 == 0, jnp.logical_and(late_s >= EARLY, late_s < NS))

        @pl.when(jnp.logical_or(ahead, follow))
        def _():
            relay_down(jnp.where(ahead, t + 2, late_s))

    loop(NJ + 9, r_tick)

    def drain(s):
        gw.drain(s)
        dw.drain(s)
        for d in range(2):
            s1(s, d).wait_send()
            s2(s, d).wait_send()
            for dx in range(2):
                a1(s, dx, d).wait_send()
                a2(s, dx, d).wait_send()
        for n in range(3):
            a3(s, n).wait_send()
            og(s, n).wait_send()
            ig(s, n).wait_send()
        z1_done(s).wait_send()
        z2_done(s).wait_send()
        for par in range(2):
            cross(s, par).wait_send()
            cross(s, par).wait_recv()

    loop(NS, drain)
    for n in range(2):
        ex(n, 0).wait_send()
        ex(n, 1).wait_send()


def on_device(tokens, routes, route_weights, w_gate, w_down):
    ids = jnp.arange(EXPERTS, dtype=jnp.int32)[:, None, None]
    wt = jnp.sum(jnp.where(routes.T[None] == ids, route_weights.T[None], 0.0), 1)
    dma = pltpu.SemaphoreType.DMA
    sems = (
        [dma((NS, 2))] + [dma((NS,))] * 14 + [dma, dma]
        + [dma((NS, 2))] * 4 + [dma((NS, 3))] * 4 + [dma((2, 2))] * 2
        + [dma((NS, 2, 2))] * 4 + [dma((NS, 3))] * 2 + [dma((NS,))] * 5 + [dma((NS, 2))] * 2
    )
    return pl.pallas_call(
        kernel,
        out_shape=jax.ShapeDtypeStruct((ROWS, D), BF),
        in_specs=[pl.BlockSpec(memory_space=pltpu.VMEM)] + [pl.BlockSpec(memory_space=pl.ANY)] * 3,
        out_specs=pl.BlockSpec(memory_space=pl.ANY),
        scratch_shapes=[
            pltpu.VMEM((NS, 2, 2, 4, ROWS, HW), BF),
            pltpu.VMEM((NS, 2, 2, 4, ROWS, HW), BF),
            pltpu.VMEM((NS, 4, FFP, CW), BF),
            pltpu.VMEM((NS, 4, FFP, CW), BF),
            pltpu.VMEM((2, 8 * ROWS, PAIR), F32),
            pltpu.VMEM((2, 8, CAP, PAIR), BF),
            pltpu.VMEM((2, 8, CAP, PAIR), BF),
            pltpu.VMEM((8 * ROWS, 2 * PAIR), BF),
            pltpu.VMEM((8, EXPERTS, ROWS), F32),
            pltpu.VMEM((8, 2, CAP, ROWS), BF),
            pltpu.VMEM((NS, 2, 2, ROWS, HW), BF),
            pltpu.VMEM((NS, 2, 2, 2, ROWS, HW), BF),
            pltpu.VMEM((NS, 3, ROWS, HW), BF),
            pltpu.VMEM((NS, 7, 32, HW), BF),
            pltpu.VMEM((NS, 32, HW), BF),
        ] + sems,
        compiler_params=pltpu.CompilerParams(
            collective_id=0, has_side_effects=True, vmem_limit_bytes=58 << 20
        ),
        cost_estimate=pl.CostEstimate(
            flops=8 * 8 * ROWS * FF * D, bytes_accessed=4 * FF * D * 2, transcendentals=32 * ROWS * FF
        ),
        name="moe",
    )(wt, tokens, w_gate, w_down)


def solution(mesh):
    in_specs = (
        P("expert", None),
        P("expert", None),
        P("expert", None),
        P("expert", "cuts", None),
        P("expert", "cuts", None),
    )
    return jax.shard_map(
        on_device, mesh=mesh, in_specs=in_specs, out_specs=P("expert", None), check_vma=False
    )
```

```python
import jax
import jax.numpy as jnp
from jax import lax
from jax.experimental import pallas as pl
from jax.experimental.pallas import tpu as pltpu
from jax.sharding import PartitionSpec as P

MESH = pl.DeviceIdType.MESH
BF = jnp.bfloat16
F32 = jnp.float32

D = 6144
HALF = D // 2
FF = 336
FFP = 384
PAIR = 2 * FFP
ROWS = 128
EXPERTS = 16
NS = 6
CW = HALF // NS
HW = CW // 2
NX = 1
XFIRST = 3
NY = NS - NX
NJ = 2 * NY
EARLY = 3
LAGS = (3, 5, 7, 9)
XTICKS = ((4, 8, 9, 11, 13, 15),)
NT = 19
LATE = 5
CAP = 64
RSLOT = {0: 0, 1: 1, 3: 2, 2: 3}


def kernel(
    wt_ref, tok_ref, wg_ref, wd_ref, o_ref,
    xp, pb, wg, wd, pre, es, er, hid, wt, pick,
    ry1, ry2, rx, qx, qy1, qy2, tz, fz,
    tok_sem,
    wgo, wgs, wgr, wgzs, wgzr, wgls, wglr,
    wdo, wds, wdr, wdzs, wdzr, wdls, wdlr,
    wts, wtr,
    s1s, s1r, s2s, s2r, os_, or_, is_, ir_, exs, exr,
    y1s, y1r, y2s, y2r, xs_, xr_,
    b1s, b1r, b2s, b2r, b3s, b3r,
    z1s, z1r, ags, agr, aglo, ils, ilr,
):
    e = lax.axis_index("expert")
    c = lax.axis_index("cuts")
    hi, y, k = e // 8, (e // 2) % 4, e % 2
    z, lo = c // 2, c % 2
    ol = 1 - lo
    zpar, zi = z % 2, z // 2

    def dev(hi_, y_, k_, z_, lo_):
        return (hi_ * 8 + y_ * 2 + k_, z_ * 2 + lo_)

    yp = dev(hi, (y + 1) % 4, k, z, lo)
    ym = dev(hi, (y + 3) % 4, k, z, lo)
    inner = dev(hi, y, k, z, ol)
    outer = dev(1 - hi, y, k, z, ol)
    across = dev(1 - hi, y, k, z, lo)
    core = dev(hi, y, 1 - k, z, lo)

    def zdev(dz, lo_):
        return dev(hi, y, k, (z + dz + 8) % 8, lo_)

    def rel(dx, dy):
        if dx == 0:
            return dev(hi, (y + dy) % 4, k, z, lo)
        return dev(1 - hi, (y + dy) % 4, k, z, ol)

    def remote(src, dst, ss, rs, to):
        return pltpu.make_async_remote_copy(
            src_ref=src, dst_ref=dst, send_sem=ss, recv_sem=rs, device_id=to, device_id_type=MESH
        )

    def cols(par, s):
        return pl.ds(pl.multiple_of(par * HALF + s * CW, CW), CW)

    def load_tok(s, h):
        at = pl.multiple_of(zpar * HALF + s * CW + h * HW, HW)
        return pltpu.make_async_copy(tok_ref.at[:, pl.ds(at, HW)], xp.at[s, h, 0, 0], tok_sem.at[s, h])

    real = pl.ds(0, FF)
    own_q, far_q = 3 * k, 2 - k

    class Weights:
        def __init__(self, src, dst, so, ss, sr, zs, zr, ls, lr):
            self.src, self.dst = src, dst
            self.so, self.ss, self.sr, self.zs, self.zr, self.ls, self.lr = so, ss, sr, zs, zr, ls, lr

        def local(self, s):
            return pltpu.make_async_copy(
                self.src.at[0, :, cols(zpar, s)], self.dst.at[s, own_q, real], self.so.at[s]
            )

        def swap(self, s):
            return remote(
                self.src.at[0, :, cols(zpar, s)], self.dst.at[s, own_q, real], self.ss.at[s], self.sr.at[s], core
            )

        def along(self, s):
            return remote(
                self.src.at[0, :, cols(1 - zpar, s)], self.dst.at[s, far_q, real],
                self.zs.at[s], self.zr.at[s], zdev(1 - 2 * k, lo),
            )

        def relay(self, s):
            ref = self.dst.at[s, far_q, real]
            return remote(ref, ref, self.ls.at[s], self.lr.at[s], core)

        def ready(self, s):
            self.local(s).wait()
            self.swap(s).wait_recv()
            self.relay(s).wait_recv()

        def drain(self, s):
            self.swap(s).wait_send()
            self.along(s).wait_send()
            self.relay(s).wait_send()

    gw = Weights(wg_ref, wg, wgo, wgs, wgr, wgzs, wgzr, wgls, wglr)
    dw = Weights(wd_ref, wd, wdo, wds, wdr, wdzs, wdzr, wdls, wdlr)

    def loop(n, body):
        def step(i, _):
            body(i)
            return 0

        lax.fori_loop(0, n, step, 0)

    def start_tok(s):
        load_tok(s, 0).start()
        load_tok(s, 1).start()

    def start_local(s):
        gw.local(s).start()
        dw.local(s).start()

    loop(NS, start_tok)

    bar = pltpu.get_barrier_semaphore()
    partners = [core]
    for dx in range(2):
        for dy in range(4):
            if (dx, dy) != (0, 0):
                partners.append(rel(dx, dy))
    for dz in range(1, 8):
        partners.append(zdev(dz, lo))
        partners.append(zdev(dz, ol))
    partners += [inner, across]
    for p in partners:
        pl.semaphore_signal(bar, inc=1, device_id=p, device_id_type=MESH)
    loop(NS, start_local)
    wt[0] = wt_ref[...]

    def clear_pad(s):
        for q in range(4):
            wg[s, q, FF:FFP, :] = jnp.zeros((FFP - FF, CW), BF)
            wd[s, q, FF:FFP, :] = jnp.zeros((FFP - FF, CW), BF)

    loop(NS, clear_pad)
    pl.semaphore_wait(bar, len(partners))

    def s1(j, d):
        return remote(
            xp.at[j, :, 0, 0], xp.at[j, :, 0, 2 - d], s1s.at[j, d], s1r.at[j, d], yp if d == 0 else ym
        )

    def s2(j, d):
        return remote(
            xp.at[j, d, 0, 2 - d], xp.at[j, d, 0, 3], s2s.at[j, d], s2r.at[j, d], yp if d == 0 else ym
        )

    part = (pl.ds(0, 1), pl.ds(1, 2), pl.ds(3, 1))

    def og(j, n):
        return remote(xp.at[j, lo, 0, part[n]], xp.at[j, lo, 1, part[n]], os_.at[j, n], or_.at[j, n], outer)

    def ig(j, n):
        ref = xp.at[j, ol, 1, part[n]]
        return remote(ref, ref, is_.at[j, n], ir_.at[j, n], inner)

    def gate(j, dx, r0, nr):
        m = nr * ROWS
        row0 = (dx * 4 + r0) * ROWS

        @pl.loop(0, 2)
        def _(i):
            acc = pre[i, row0:row0 + m, :]
            for h in range(2):
                xs = xp[j, h, dx, r0:r0 + nr].reshape(m, HW)
                ws = wg[j, pl.ds(2 * i, 2), :, h * HW:(h + 1) * HW].reshape(PAIR, HW)
                acc = acc + lax.dot_general(xs, ws, (((1,), (1,)), ((), ())), preferred_element_type=F32)
            pre[i, row0:row0 + m, :] = acc

    def ex(n, d):
        blocks = pl.ds(4 * n, 4)
        return remote(es.at[d, blocks], er.at[d, blocks], exs.at[n, d], exr.at[n, d], zdev(1 - 2 * d, lo))

    def exchange(n):
        def stage(i):
            b = 4 * n + i
            rows = pl.ds(pl.multiple_of(b * ROWS, ROWS), ROWS)
            for d in range(2):
                for q in range(2):
                    v = pre[d, rows, q * FFP:(q + 1) * FFP].astype(BF)
                    es[d, b, :, q * FFP:(q + 1) * FFP] = jnp.dot(
                        pick[b, q], v, preferred_element_type=F32
                    ).astype(BF)

        loop(4, stage)
        ex(n, 0).start()
        ex(n, 1).start()

    e0 = 2 * (e // 2)

    def make_pick():
        got = wt.at[pl.ds(1, 7)]
        all_wt = remote(got, got, wts, wtr, core)
        all_wt.wait_send()
        all_wt.wait_recv()
        ri = lax.broadcasted_iota(jnp.int32, (ROWS, ROWS), 0)
        ci = lax.broadcasted_iota(jnp.int32, (ROWS, ROWS), 1)
        upto = jnp.where(ri <= ci, 1.0, 0.0).astype(BF)
        row = lax.broadcasted_iota(jnp.int32, (EXPERTS, ROWS), 0)
        slot = lax.broadcasted_iota(jnp.int32, (CAP, ROWS), 0).astype(F32)

        def block(b):
            hit = jnp.where(wt[b] > 0.0, 1.0, 0.0)
            place = jnp.dot(hit.astype(BF), upto, preferred_element_type=F32) * hit - 1.0
            for q in range(2):
                mine = jnp.sum(jnp.where(row == e0 + q, place, 0.0), axis=0, keepdims=True)
                pick[b, q] = jnp.where(slot == mine, 1.0, 0.0).astype(BF)

        loop(8, block)

    def send_own(j):
        load_tok(j, 0).wait()
        load_tok(j, 1).wait()
        s1(j, 0).start()
        s1(j, 1).start()
        og(j, 0).start()

    def swap_gate(j):
        gw.swap(j).start()

    for j in range(2):
        gw.along(j).start()
        send_own(j)
    loop(NS, swap_gate)
    for dx in range(2):
        for dy in range(4):
            if (dx, dy) != (0, 0):
                remote(wt_ref, wt.at[dx * 4 + RSLOT[(4 - dy) % 4]], wts, wtr, rel(dx, dy)).start()

    def clear_pre(b):
        rows = pl.ds(pl.multiple_of(b * ROWS, ROWS), ROWS)
        for i in range(2):
            pre[i, rows, :] = jnp.zeros((ROWS, PAIR), F32)

    loop(8, clear_pre)

    def at(t, lag):
        return jnp.logical_and(t >= lag, t < NS + lag)

    def g_tick(t):
        @pl.when(t < NS)
        def _():
            s1(t, 0).wait_recv()
            s2(t, 0).start()
            s1(t, 1).wait_recv()
            s2(t, 1).start()
            og(t, 1).start()

        @pl.when(t + 2 < NS)
        def _():
            send_own(t + 2)
            gw.along(t + 2).start()

        @pl.when(jnp.logical_and(t >= 3, t < 6))
        def _():
            dw.along(t - 3).start()

        @pl.when(t < NS)
        def _():
            og(t, 0).wait_recv()
            ig(t, 0).start()
            dw.swap(t).start()

        @pl.when(at(t, 1))
        def _():
            s2(t - 1, 0).wait_recv()
            s2(t - 1, 1).wait_recv()
            og(t - 1, 2).start()

        @pl.when(at(t, 2))
        def _():
            og(t - 2, 1).wait_recv()
            ig(t - 2, 1).start()

        @pl.when(at(t, 3))
        def _():
            og(t - 3, 2).wait_recv()
            ig(t - 3, 2).start()

        @pl.when(t < NS)
        def _():
            gw.along(t).wait_recv()
            gw.relay(t).start()

        @pl.when(t == 2)
        def _():
            make_pick()

        @pl.when(at(t, 1))
        def _():
            gw.ready(t - 1)
            gate(t - 1, 0, 0, 4)

        @pl.when(t == NS)
        def _():
            exchange(0)

        @pl.when(at(t, 4))
        def _():
            for n in range(3):
                ig(t - 4, n).wait_recv()
            gate(t - 4, 1, 0, 4)

    loop(NS + 4, g_tick)
    exchange(1)

    def relay_down(s):
        dw.along(s).wait_recv()
        dw.relay(s).start()

    relay_down(0)

    col = lax.broadcasted_iota(jnp.int32, (EXPERTS, PAIR), 1)
    row = lax.broadcasted_iota(jnp.int32, (EXPERTS, PAIR), 0)
    hit0 = jnp.logical_and(row == e0, col < FF)
    hit1 = jnp.logical_and(row == e0 + 1, jnp.logical_and(col >= FFP, col < FFP + FF))
    sel = jnp.where(jnp.logical_or(hit0, hit1), 1.0, 0.0).astype(F32)

    def hidden(b):
        rows = pl.ds(pl.multiple_of(b * ROWS, ROWS), ROWS)
        scale = lax.dot_general(
            wt[b], sel, (((0,), (0,)), ((), ())),
            preferred_element_type=F32, precision=lax.Precision.HIGHEST,
        )
        for i in range(2):
            for q in range(2):
                at = slice(q * FFP, (q + 1) * FFP)
                more = lax.dot_general(
                    pick[b, q], er[1 - i, b, :, at], (((0,), (0,)), ((), ())), preferred_element_type=F32
                )
                v = pre[i, rows, at] + more
                to = i * PAIR + q * FFP
                hid[rows, to:to + FFP] = (scale[:, at] * (v / (1.0 + jnp.exp(-v)))).astype(BF)

    ex(0, 0).wait_recv()
    ex(0, 1).wait_recv()
    loop(4, hidden)
    relay_down(1)

    def down(s, dx):
        @pl.loop(0, 2)
        def _(i):
            rows = pl.ds(pl.multiple_of(dx * 512 + i * 256, 256), 256)
            r = jnp.dot(hid[rows, :], wd[s].reshape(4 * FFP, CW), preferred_element_type=F32).astype(BF)
            for h in range(2):
                pb[s, h, dx, pl.ds(i * 2, 2)] = r[:, h * HW:(h + 1) * HW].reshape(2, ROWS, HW)

    def total(*parts):
        acc = parts[0].astype(F32)
        for p in parts[1:]:
            acc = acc + p.astype(F32)
        return acc.astype(BF)

    def ychunk(i):
        return jnp.where(i < XFIRST, i, i + NX)

    def yto(d):
        return yp if d == 0 else ym

    def a1(i, dx, d):
        return remote(pb.at[ychunk(i), d, dx, 3], ry1.at[i, dx, d], y1s.at[i, dx, d], y1r.at[i, dx, d], yto(d))

    def a2(i, dx, d):
        return remote(
            pb.at[ychunk(i), :, dx, 1 + d], ry2.at[i, dx, d], y2s.at[i, dx, d], y2r.at[i, dx, d], yto(d)
        )

    def a3(i, n):
        s = ychunk(i)
        src = pb.at[s, ol, n, 0] if n < 2 else pb.at[s, lo, 1, 0]
        return remote(src, rx.at[i, n], xs_.at[i, n], xr_.at[i, n], (inner, outer, across)[n])

    half = (pl.ds(0, 64), pl.ds(64, 64))

    def b1(i, n):
        s = XFIRST + i
        src = pb.at[s, ol, n] if n < 2 else pb.at[s, lo, 1]
        return remote(src, qx.at[i, n], b1s.at[i, n], b1r.at[i, n], (inner, outer, across)[n])

    def b2(i, d):
        return remote(
            pb.at[XFIRST + i, lo, 0, 3, half[d]], qy1.at[i, d], b2s.at[i, d], b2r.at[i, d], yto(d)
        )

    def b3(i, d):
        return remote(pb.at[XFIRST + i, lo, 0, 1 + d], qy2.at[i, d], b3s.at[i, d], b3r.at[i, d], yto(d))

    def z1(s):
        for dz in range(1, 4):
            remote(
                tz.at[s, (zi + dz) % 4], tz.at[s, 4 + (3 - dz)], z1s.at[s], z1r.at[s], zdev(2 * dz, lo)
            ).start()

    def z1_done(s):
        ref = tz.at[s, pl.ds(4, 3)]
        return remote(ref, ref, z1s.at[s], z1r.at[s], core)

    def place(s, lo_):
        return o_ref.at[
            pl.ds(pl.multiple_of(zi * 32, 32), 32),
            pl.ds(pl.multiple_of(zpar * HALF + s * CW + lo_ * HW, HW), HW),
        ]

    def keep(s):
        return pltpu.make_async_copy(fz.at[s], place(s, lo), aglo.at[s])

    def z2(s):
        keep(s).start()
        for dz in range(1, 8):
            remote(fz.at[s], place(s, lo), ags.at[s], agr.at[s], zdev(dz, lo)).start()

        @pl.when(s >= LATE)
        def _():
            for dz in range(8):
                remote(fz.at[s], place(s, lo), ils.at[s, dz % 2], ilr.at[s, zpar], zdev(dz, ol)).start()

    def cross(s, par):
        at = pl.multiple_of(par * HALF + s * CW + lo * HW, HW)
        ref = o_ref.at[:, pl.ds(at, HW)]
        return remote(ref, ref, ils.at[s, par], ilr.at[s, par], inner)

    def z3(s):
        keep(s).wait()
        z2_done(s).wait_recv()

        @pl.when(s < LATE)
        def _():
            cross(s, 0).start()
            cross(s, 1).start()

    def z2_done(s):
        return remote(tz.at[s], tz.at[s], ags.at[s], agr.at[s], core)

    def job(t):
        early = t < 2 * EARLY
        return jnp.where(early, t % EARLY, t // 2), jnp.where(early, t // EARLY, t % 2)

    def r_tick(t):
        @pl.when(t == EARLY)
        def _():
            ex(1, 0).wait_recv()
            ex(1, 1).wait_recv()
            dw.along(3).start()
            dw.along(4).start()
            dw.along(5).start()

            def late(b):
                hidden(b + 4)

            loop(4, late)

        @pl.when(t < NJ)
        def _():
            i, dx = job(t)
            s = ychunk(i)

            @pl.when(dx == 0)
            def _():
                dw.ready(s)

            down(s, dx)
            a1(i, dx, 0).start()
            a1(i, dx, 1).start()

        @pl.when(jnp.logical_and(t >= 1, t - 1 < NJ))
        def _():
            i, dx = job(t - 1)
            s = ychunk(i)
            for d in range(2):
                a1(i, dx, d).wait_recv()
                pb[s, d, dx, 1 + d] = total(pb[s, d, dx, 1 + d], ry1[i, dx, d])
                a2(i, dx, d).start()

        @pl.when(jnp.logical_and(t >= LAGS[0], t - LAGS[0] < NJ))
        def _():
            i, dx = job(t - LAGS[0])
            s = ychunk(i)
            a2(i, dx, 0).wait_recv()
            a2(i, dx, 1).wait_recv()
            pb[s, :, dx, 0] = total(pb[s, :, dx, 0], ry2[i, dx, 0], ry2[i, dx, 1])

        def stage(n, fn):
            u = t - EARLY - n
            near = jnp.logical_and(u >= 0, u < EARLY)
            i = jnp.where(near, u, (u + EARLY - 1) // 2)
            far = jnp.logical_and((u + EARLY - 1) % 2 == 0, jnp.logical_and(u > EARLY, i < NY))

            @pl.when(jnp.logical_or(near, far))
            def _():
                fn(i)

        def go_x(i):
            for n in range(3):
                a3(i, n).start()

        def go_z1(i):
            s = ychunk(i)
            for n in range(3):
                a3(i, n).wait_recv()
            tz[s, 0:4] = total(pb[s, lo, 0, 0], rx[i, 0], rx[i, 1], rx[i, 2]).reshape(4, 32, HW)
            z1(s)

        def sum_z(s):
            z1_done(s).wait_recv()
            fz[s] = total(tz[s, zi], tz[s, 4], tz[s, 5], tz[s, 6])
            z2(s)

        def go_z2(i):
            sum_z(ychunk(i))

        def go_z3(i):
            z3(ychunk(i))

        def x_first(i):
            s = XFIRST + i
            dw.ready(s)
            down(s, 1)
            b1(i, 1).start()
            b1(i, 2).start()
            down(s, 0)
            b1(i, 0).start()

        def x_sum(i):
            s = XFIRST + i
            for n in range(3):
                b1(i, n).wait_recv()
            for r in (3, 1, 2, 0):
                pb[s, lo, 0, r] = total(pb[s, lo, 0, r], qx[i, 0, r], qx[i, 1, r], qx[i, 2, r])
                if r == 3:
                    b2(i, 0).start()
                    b2(i, 1).start()

        def x_y2(i):
            s = XFIRST + i
            for d in range(2):
                b2(i, d).wait_recv()
                rows = slice(64 * d, 64 * d + 64)
                pb[s, lo, 0, 1 + d, rows] = total(pb[s, lo, 0, 1 + d, rows], qy1[i, d])
                b3(i, d).start()

        def x_z1(i):
            s = XFIRST + i
            b3(i, 0).wait_recv()
            b3(i, 1).wait_recv()
            tz[s, 0:4] = total(pb[s, lo, 0, 0], qy2[i, 0], qy2[i, 1]).reshape(4, 32, HW)
            z1(s)

        def x_z2(i):
            sum_z(XFIRST + i)

        def x_z3(i):
            z3(XFIRST + i)

        steps = (x_first, x_sum, x_y2, x_z1, x_z2, x_z3)
        stage(LAGS[0], go_x)
        stage(LAGS[1], go_z1)
        stage(LAGS[2], go_z2)
        stage(LAGS[3], go_z3)
        for i in range(NX):
            for fn, when in zip(steps, XTICKS[i]):
                @pl.when(t == when)
                def _(fn=fn, i=i):
                    fn(i)

        @pl.when(t == 0)
        def _():
            relay_down(2)

        @pl.when(jnp.logical_and(t >= 3, t < 6))
        def _():
            relay_down(t)

    loop(NT, r_tick)

    def drain(s):
        gw.drain(s)
        dw.drain(s)
        for d in range(2):
            s1(s, d).wait_send()
            s2(s, d).wait_send()
        for n in range(3):
            og(s, n).wait_send()
            ig(s, n).wait_send()
        z1_done(s).wait_send()
        z2_done(s).wait_send()
        for par in range(2):
            cross(s, par).wait_send()
            cross(s, par).wait_recv()

    loop(NS, drain)

    def drain_y(i):
        for n in range(3):
            a3(i, n).wait_send()
        for dx in range(2):
            for d in range(2):
                a1(i, dx, d).wait_send()
                a2(i, dx, d).wait_send()

    def drain_x(i):
        for n in range(3):
            b1(i, n).wait_send()
        for d in range(2):
            b2(i, d).wait_send()
            b3(i, d).wait_send()

    loop(NY, drain_y)
    loop(NX, drain_x)
    for n in range(2):
        ex(n, 0).wait_send()
        ex(n, 1).wait_send()


def on_device(tokens, routes, route_weights, w_gate, w_down):
    ids = jnp.arange(EXPERTS, dtype=jnp.int32)[:, None, None]
    wt = jnp.sum(jnp.where(routes.T[None] == ids, route_weights.T[None], 0.0), 1)
    dma = pltpu.SemaphoreType.DMA
    sems = (
        [dma((NS, 2))] + [dma((NS,))] * 14 + [dma, dma]
        + [dma((NS, 2))] * 4 + [dma((NS, 3))] * 4 + [dma((2, 2))] * 2
        + [dma((NY, 2, 2))] * 4 + [dma((NY, 3))] * 2
        + [dma((NX, 3))] * 2 + [dma((NX, 2))] * 4
        + [dma((NS,))] * 5 + [dma((NS, 2))] * 2
    )
    return pl.pallas_call(
        kernel,
        out_shape=jax.ShapeDtypeStruct((ROWS, D), BF),
        in_specs=[pl.BlockSpec(memory_space=pltpu.VMEM)] + [pl.BlockSpec(memory_space=pl.ANY)] * 3,
        out_specs=pl.BlockSpec(memory_space=pl.ANY),
        scratch_shapes=[
            pltpu.VMEM((NS, 2, 2, 4, ROWS, HW), BF),
            pltpu.VMEM((NS, 2, 2, 4, ROWS, HW), BF),
            pltpu.VMEM((NS, 4, FFP, CW), BF),
            pltpu.VMEM((NS, 4, FFP, CW), BF),
            pltpu.VMEM((2, 8 * ROWS, PAIR), F32),
            pltpu.VMEM((2, 8, CAP, PAIR), BF),
            pltpu.VMEM((2, 8, CAP, PAIR), BF),
            pltpu.VMEM((8 * ROWS, 2 * PAIR), BF),
            pltpu.VMEM((8, EXPERTS, ROWS), F32),
            pltpu.VMEM((8, 2, CAP, ROWS), BF),
            pltpu.VMEM((NY, 2, 2, ROWS, HW), BF),
            pltpu.VMEM((NY, 2, 2, 2, ROWS, HW), BF),
            pltpu.VMEM((NY, 3, ROWS, HW), BF),
            pltpu.VMEM((NX, 3, 4, ROWS, HW), BF),
            pltpu.VMEM((NX, 2, ROWS // 2, HW), BF),
            pltpu.VMEM((NX, 2, ROWS, HW), BF),
            pltpu.VMEM((NS, 7, 32, HW), BF),
            pltpu.VMEM((NS, 32, HW), BF),
        ] + sems,
        compiler_params=pltpu.CompilerParams(
            collective_id=0, has_side_effects=True, vmem_limit_bytes=58 << 20
        ),
        cost_estimate=pl.CostEstimate(
            flops=8 * 8 * ROWS * FF * D, bytes_accessed=4 * FF * D * 2, transcendentals=32 * ROWS * FF
        ),
        name="moe",
    )(wt, tokens, w_gate, w_down)


def solution(mesh):
    in_specs = (
        P("expert", None),
        P("expert", None),
        P("expert", None),
        P("expert", "cuts", None),
        P("expert", "cuts", None),
    )
    return jax.shard_map(
        on_device, mesh=mesh, in_specs=in_specs, out_specs=P("expert", None), check_vma=False
    )
```

```python
import jax
import jax.numpy as jnp
from jax import lax
from jax.experimental import pallas as pl
from jax.experimental.pallas import tpu as pltpu
from jax.sharding import PartitionSpec as P

MESH = pl.DeviceIdType.MESH
BF = jnp.bfloat16
F32 = jnp.float32

D = 6144
HALF = D // 2
FF = 336
FFP = 384
PAIR = 2 * FFP
ROWS = 128
EXPERTS = 16
NS = 6
CW = HALF // NS
HW = CW // 2
LAST = NS - 1
NX = 1
XFIRST = 3
NY = NS - NX
NJ = 2 * NY
EARLY = 3
LAGS = (3, 5, 7, 9)
XTICKS = ((4, 8, 9, 11, 13, 15),)
NT = 19
LATE = 5
CAP = 64
RSLOT = {0: 0, 1: 1, 3: 2, 2: 3}


def kernel(
    wt_ref, tok_ref, wg_ref, wd_ref, o_ref,
    xp, pb, wg, wd, pre, es, er, hid, wt, pick,
    ry1, ry2, rx, qx, qy1, qy2, tz, fz,
    tok_sem,
    wgo, wgs, wgr, wgzs, wgzr, wgls, wglr,
    wdo, wds, wdr, wdzs, wdzr, wdls, wdlr,
    wts, wtr,
    s1s, s1r, s2s, s2r, p1s, p1r, p2s, p2r, os_, or_, is_, ir_, exs, exr,
    y1s, y1r, y2s, y2r, xs_, xr_,
    b1s, b1r, b2s, b2r, b3s, b3r,
    z1s, z1r, ags, agr, aglo, ils, ilr,
):
    e = lax.axis_index("expert")
    c = lax.axis_index("cuts")
    hi, y, k = e // 8, (e // 2) % 4, e % 2
    z, lo = c // 2, c % 2
    ol = 1 - lo
    zpar, zi = z % 2, z // 2

    def dev(hi_, y_, k_, z_, lo_):
        return (hi_ * 8 + y_ * 2 + k_, z_ * 2 + lo_)

    yp = dev(hi, (y + 1) % 4, k, z, lo)
    ym = dev(hi, (y + 3) % 4, k, z, lo)
    inner = dev(hi, y, k, z, ol)
    outer = dev(1 - hi, y, k, z, ol)
    across = dev(1 - hi, y, k, z, lo)
    core = dev(hi, y, 1 - k, z, lo)

    def zdev(dz, lo_):
        return dev(hi, y, k, (z + dz + 8) % 8, lo_)

    def rel(dx, dy):
        if dx == 0:
            return dev(hi, (y + dy) % 4, k, z, lo)
        return dev(1 - hi, (y + dy) % 4, k, z, ol)

    def remote(src, dst, ss, rs, to):
        return pltpu.make_async_remote_copy(
            src_ref=src, dst_ref=dst, send_sem=ss, recv_sem=rs, device_id=to, device_id_type=MESH
        )

    def cols(par, s):
        return pl.ds(pl.multiple_of(par * HALF + s * CW, CW), CW)

    def load_tok(s, h):
        at = pl.multiple_of(zpar * HALF + s * CW + h * HW, HW)
        return pltpu.make_async_copy(tok_ref.at[:, pl.ds(at, HW)], xp.at[s, h, 0, 0], tok_sem.at[s, h])

    real = pl.ds(0, FF)
    own_q, far_q = 3 * k, 2 - k

    class Weights:
        def __init__(self, src, dst, so, ss, sr, zs, zr, ls, lr):
            self.src, self.dst = src, dst
            self.so, self.ss, self.sr, self.zs, self.zr, self.ls, self.lr = so, ss, sr, zs, zr, ls, lr

        def local(self, s):
            return pltpu.make_async_copy(
                self.src.at[0, :, cols(zpar, s)], self.dst.at[s, own_q, real], self.so.at[s]
            )

        def swap(self, s):
            return remote(
                self.src.at[0, :, cols(zpar, s)], self.dst.at[s, own_q, real], self.ss.at[s], self.sr.at[s], core
            )

        def along(self, s):
            return remote(
                self.src.at[0, :, cols(1 - zpar, s)], self.dst.at[s, far_q, real],
                self.zs.at[s], self.zr.at[s], zdev(1 - 2 * k, lo),
            )

        def relay(self, s):
            ref = self.dst.at[s, far_q, real]
            return remote(ref, ref, self.ls.at[s], self.lr.at[s], core)

        def ready(self, s):
            self.local(s).wait()
            self.swap(s).wait_recv()
            self.relay(s).wait_recv()

        def drain(self, s):
            self.swap(s).wait_send()
            self.along(s).wait_send()
            self.relay(s).wait_send()

    gw = Weights(wg_ref, wg, wgo, wgs, wgr, wgzs, wgzr, wgls, wglr)
    dw = Weights(wd_ref, wd, wdo, wds, wdr, wdzs, wdzr, wdls, wdlr)

    def loop(n, body):
        def step(i, _):
            body(i)
            return 0

        lax.fori_loop(0, n, step, 0)

    def start_tok(s):
        load_tok(s, 0).start()
        load_tok(s, 1).start()

    def start_local(s):
        gw.local(s).start()
        dw.local(s).start()

    loop(NS, start_tok)

    bar = pltpu.get_barrier_semaphore()
    partners = [core]
    for dx in range(2):
        for dy in range(4):
            if (dx, dy) != (0, 0):
                partners.append(rel(dx, dy))
    for dz in range(1, 8):
        partners.append(zdev(dz, lo))
        partners.append(zdev(dz, ol))
    partners += [inner, across]
    for p in partners:
        pl.semaphore_signal(bar, inc=1, device_id=p, device_id_type=MESH)
    loop(NS, start_local)
    wt[0] = wt_ref[...]

    def clear_pad(s):
        for q in range(4):
            wg[s, q, FF:FFP, :] = jnp.zeros((FFP - FF, CW), BF)
            wd[s, q, FF:FFP, :] = jnp.zeros((FFP - FF, CW), BF)

    loop(NS, clear_pad)
    pl.semaphore_wait(bar, len(partners))

    def s1(j, d):
        return remote(
            xp.at[j, :, 0, 0], xp.at[j, :, 0, 2 - d], s1s.at[j, d], s1r.at[j, d], yp if d == 0 else ym
        )

    def s2(j, d):
        return remote(
            xp.at[j, d, 0, 2 - d], xp.at[j, d, 0, 3], s2s.at[j, d], s2r.at[j, d], yp if d == 0 else ym
        )

    def p1(d):
        return remote(
            xp.at[LAST, :, 1, 0], xp.at[LAST, :, 1, 2 - d], p1s.at[d], p1r.at[d], yp if d == 0 else ym
        )

    def p2(d):
        return remote(
            xp.at[LAST, d, 1, 2 - d], xp.at[LAST, d, 1, 3], p2s.at[d], p2r.at[d], yp if d == 0 else ym
        )

    part = (pl.ds(0, 1), pl.ds(1, 2), pl.ds(3, 1))

    def og(j, n):
        return remote(xp.at[j, lo, 0, part[n]], xp.at[j, lo, 1, part[n]], os_.at[j, n], or_.at[j, n], outer)

    def ig(j, n):
        ref = xp.at[j, ol, 1, part[n]]
        return remote(ref, ref, is_.at[j, n], ir_.at[j, n], inner)

    def gate(j, dx, r0, nr):
        m = nr * ROWS
        row0 = (dx * 4 + r0) * ROWS

        @pl.loop(0, 2)
        def _(i):
            acc = pre[i, row0:row0 + m, :]
            for h in range(2):
                xs = xp[j, h, dx, r0:r0 + nr].reshape(m, HW)
                ws = wg[j, pl.ds(2 * i, 2), :, h * HW:(h + 1) * HW].reshape(PAIR, HW)
                acc = acc + lax.dot_general(xs, ws, (((1,), (1,)), ((), ())), preferred_element_type=F32)
            pre[i, row0:row0 + m, :] = acc

    def ex(n, d):
        blocks = pl.ds(4 * n, 4)
        return remote(es.at[d, blocks], er.at[d, blocks], exs.at[n, d], exr.at[n, d], zdev(1 - 2 * d, lo))

    def exchange(n):
        def stage(i):
            b = 4 * n + i
            rows = pl.ds(pl.multiple_of(b * ROWS, ROWS), ROWS)
            for d in range(2):
                for q in range(2):
                    v = pre[d, rows, q * FFP:(q + 1) * FFP].astype(BF)
                    es[d, b, :, q * FFP:(q + 1) * FFP] = jnp.dot(
                        pick[b, q], v, preferred_element_type=F32
                    ).astype(BF)

        loop(4, stage)
        ex(n, 0).start()
        ex(n, 1).start()

    e0 = 2 * (e // 2)

    def make_pick():
        got = wt.at[pl.ds(1, 7)]
        all_wt = remote(got, got, wts, wtr, core)
        all_wt.wait_send()
        all_wt.wait_recv()
        ri = lax.broadcasted_iota(jnp.int32, (ROWS, ROWS), 0)
        ci = lax.broadcasted_iota(jnp.int32, (ROWS, ROWS), 1)
        upto = jnp.where(ri <= ci, 1.0, 0.0).astype(BF)
        row = lax.broadcasted_iota(jnp.int32, (EXPERTS, ROWS), 0)
        slot = lax.broadcasted_iota(jnp.int32, (CAP, ROWS), 0).astype(F32)

        def block(b):
            hit = jnp.where(wt[b] > 0.0, 1.0, 0.0)
            place = jnp.dot(hit.astype(BF), upto, preferred_element_type=F32) * hit - 1.0
            for q in range(2):
                mine = jnp.sum(jnp.where(row == e0 + q, place, 0.0), axis=0, keepdims=True)
                pick[b, q] = jnp.where(slot == mine, 1.0, 0.0).astype(BF)

        loop(8, block)

    def send_out(j):
        load_tok(j, 0).wait()
        load_tok(j, 1).wait()
        og(j, 0).start()

    def send_own(j):
        s1(j, 0).start()
        s1(j, 1).start()

    def swap_gate(j):
        gw.swap(j).start()

    for j in range(2):
        gw.along(j).start()
        send_out(j)
        send_own(j)
    send_out(LAST)
    loop(NS, swap_gate)
    for dx in range(2):
        for dy in range(4):
            if (dx, dy) != (0, 0):
                remote(wt_ref, wt.at[dx * 4 + RSLOT[(4 - dy) % 4]], wts, wtr, rel(dx, dy)).start()

    def clear_pre(b):
        rows = pl.ds(pl.multiple_of(b * ROWS, ROWS), ROWS)
        for i in range(2):
            pre[i, rows, :] = jnp.zeros((ROWS, PAIR), F32)

    loop(8, clear_pre)

    def at(t, lag, n=NS):
        return jnp.logical_and(t >= lag, t < n + lag)

    def g_tick(t):
        @pl.when(t < NS)
        def _():
            s1(t, 0).wait_recv()
            s2(t, 0).start()
            s1(t, 1).wait_recv()
            s2(t, 1).start()

        @pl.when(t < LAST)
        def _():
            og(t, 1).start()

        @pl.when(t + 2 < LAST)
        def _():
            send_out(t + 2)

        @pl.when(t + 2 < NS)
        def _():
            send_own(t + 2)
            gw.along(t + 2).start()

        @pl.when(jnp.logical_and(t >= 3, t < 6))
        def _():
            dw.along(t - 3).start()

        @pl.when(t < LAST)
        def _():
            og(t, 0).wait_recv()
            ig(t, 0).start()

        @pl.when(t < NS)
        def _():
            dw.swap(t).start()

        @pl.when(t == 2)
        def _():
            og(LAST, 0).wait_recv()
            ig(LAST, 0).start()

        @pl.when(t == 4)
        def _():
            ig(LAST, 0).wait_recv()
            p1(0).start()
            p1(1).start()

        @pl.when(t == 5)
        def _():
            for d in range(2):
                p1(d).wait_recv()
                p2(d).start()

        @pl.when(at(t, 1))
        def _():
            s2(t - 1, 0).wait_recv()
            s2(t - 1, 1).wait_recv()

        @pl.when(at(t, 1, LAST))
        def _():
            og(t - 1, 2).start()

        @pl.when(at(t, 2, LAST))
        def _():
            og(t - 2, 1).wait_recv()
            ig(t - 2, 1).start()

        @pl.when(at(t, 3, LAST))
        def _():
            og(t - 3, 2).wait_recv()
            ig(t - 3, 2).start()

        @pl.when(t < NS)
        def _():
            gw.along(t).wait_recv()
            gw.relay(t).start()

        @pl.when(t == 2)
        def _():
            make_pick()

        @pl.when(at(t, 1))
        def _():
            gw.ready(t - 1)
            gate(t - 1, 0, 0, 4)

        @pl.when(t == NS)
        def _():
            exchange(0)

        @pl.when(t == 7)
        def _():
            p2(0).wait_recv()
            p2(1).wait_recv()
            gate(LAST, 1, 0, 4)

        @pl.when(at(t, 4, LAST))
        def _():
            for n in range(3):
                ig(t - 4, n).wait_recv()
            gate(t - 4, 1, 0, 4)

    loop(LAST + 4, g_tick)
    exchange(1)

    def relay_down(s):
        dw.along(s).wait_recv()
        dw.relay(s).start()

    relay_down(0)

    col = lax.broadcasted_iota(jnp.int32, (EXPERTS, PAIR), 1)
    row = lax.broadcasted_iota(jnp.int32, (EXPERTS, PAIR), 0)
    hit0 = jnp.logical_and(row == e0, col < FF)
    hit1 = jnp.logical_and(row == e0 + 1, jnp.logical_and(col >= FFP, col < FFP + FF))
    sel = jnp.where(jnp.logical_or(hit0, hit1), 1.0, 0.0).astype(F32)

    def hidden(b):
        rows = pl.ds(pl.multiple_of(b * ROWS, ROWS), ROWS)
        scale = lax.dot_general(
            wt[b], sel, (((0,), (0,)), ((), ())),
            preferred_element_type=F32, precision=lax.Precision.HIGHEST,
        )
        for i in range(2):
            for q in range(2):
                at = slice(q * FFP, (q + 1) * FFP)
                more = lax.dot_general(
                    pick[b, q], er[1 - i, b, :, at], (((0,), (0,)), ((), ())), preferred_element_type=F32
                )
                v = pre[i, rows, at] + more
                to = i * PAIR + q * FFP
                hid[rows, to:to + FFP] = (scale[:, at] * (v / (1.0 + jnp.exp(-v)))).astype(BF)

    ex(0, 0).wait_recv()
    ex(0, 1).wait_recv()
    loop(4, hidden)
    relay_down(1)

    def down(s, dx):
        @pl.loop(0, 2)
        def _(i):
            rows = pl.ds(pl.multiple_of(dx * 512 + i * 256, 256), 256)
            r = jnp.dot(hid[rows, :], wd[s].reshape(4 * FFP, CW), preferred_element_type=F32).astype(BF)
            for h in range(2):
                pb[s, h, dx, pl.ds(i * 2, 2)] = r[:, h * HW:(h + 1) * HW].reshape(2, ROWS, HW)

    def total(*parts):
        acc = parts[0].astype(F32)
        for p in parts[1:]:
            acc = acc + p.astype(F32)
        return acc.astype(BF)

    def ychunk(i):
        return jnp.where(i < XFIRST, i, i + NX)

    def yto(d):
        return yp if d == 0 else ym

    def a1(i, dx, d):
        return remote(pb.at[ychunk(i), d, dx, 3], ry1.at[i, dx, d], y1s.at[i, dx, d], y1r.at[i, dx, d], yto(d))

    def a2(i, dx, d):
        return remote(
            pb.at[ychunk(i), :, dx, 1 + d], ry2.at[i, dx, d], y2s.at[i, dx, d], y2r.at[i, dx, d], yto(d)
        )

    def a3(i, n):
        s = ychunk(i)
        src = pb.at[s, ol, n, 0] if n < 2 else pb.at[s, lo, 1, 0]
        return remote(src, rx.at[i, n], xs_.at[i, n], xr_.at[i, n], (inner, outer, across)[n])

    half = (pl.ds(0, 64), pl.ds(64, 64))

    def b1(i, n):
        s = XFIRST + i
        src = pb.at[s, ol, n] if n < 2 else pb.at[s, lo, 1]
        return remote(src, qx.at[i, n], b1s.at[i, n], b1r.at[i, n], (inner, outer, across)[n])

    def b2(i, d):
        return remote(
            pb.at[XFIRST + i, lo, 0, 3, half[d]], qy1.at[i, d], b2s.at[i, d], b2r.at[i, d], yto(d)
        )

    def b3(i, d):
        return remote(pb.at[XFIRST + i, lo, 0, 1 + d], qy2.at[i, d], b3s.at[i, d], b3r.at[i, d], yto(d))

    def z1(s):
        for dz in range(1, 4):
            remote(
                tz.at[s, (zi + dz) % 4], tz.at[s, 4 + (3 - dz)], z1s.at[s], z1r.at[s], zdev(2 * dz, lo)
            ).start()

    def z1_done(s):
        ref = tz.at[s, pl.ds(4, 3)]
        return remote(ref, ref, z1s.at[s], z1r.at[s], core)

    def place(s, lo_):
        return o_ref.at[
            pl.ds(pl.multiple_of(zi * 32, 32), 32),
            pl.ds(pl.multiple_of(zpar * HALF + s * CW + lo_ * HW, HW), HW),
        ]

    def keep(s):
        return pltpu.make_async_copy(fz.at[s], place(s, lo), aglo.at[s])

    def z2(s):
        keep(s).start()
        for dz in range(1, 8):
            remote(fz.at[s], place(s, lo), ags.at[s], agr.at[s], zdev(dz, lo)).start()

        @pl.when(s >= LATE)
        def _():
            for dz in range(8):
                remote(fz.at[s], place(s, lo), ils.at[s, dz % 2], ilr.at[s, zpar], zdev(dz, ol)).start()

    def cross(s, par):
        at = pl.multiple_of(par * HALF + s * CW + lo * HW, HW)
        ref = o_ref.at[:, pl.ds(at, HW)]
        return remote(ref, ref, ils.at[s, par], ilr.at[s, par], inner)

    def z3(s):
        keep(s).wait()
        z2_done(s).wait_recv()

        @pl.when(s < LATE)
        def _():
            cross(s, 0).start()
            cross(s, 1).start()

    def z2_done(s):
        return remote(tz.at[s], tz.at[s], ags.at[s], agr.at[s], core)

    def job(t):
        early = t < 2 * EARLY
        return jnp.where(early, t % EARLY, t // 2), jnp.where(early, t // EARLY, t % 2)

    def r_tick(t):
        @pl.when(t == EARLY)
        def _():
            ex(1, 0).wait_recv()
            ex(1, 1).wait_recv()
            dw.along(3).start()
            dw.along(4).start()
            dw.along(5).start()

            def late(b):
                hidden(b + 4)

            loop(4, late)

        @pl.when(t < NJ)
        def _():
            i, dx = job(t)
            s = ychunk(i)

            @pl.when(dx == 0)
            def _():
                dw.ready(s)

            down(s, dx)
            a1(i, dx, 0).start()
            a1(i, dx, 1).start()

        @pl.when(jnp.logical_and(t >= 1, t - 1 < NJ))
        def _():
            i, dx = job(t - 1)
            s = ychunk(i)
            for d in range(2):
                a1(i, dx, d).wait_recv()
                pb[s, d, dx, 1 + d] = total(pb[s, d, dx, 1 + d], ry1[i, dx, d])
                a2(i, dx, d).start()

        @pl.when(jnp.logical_and(t >= LAGS[0], t - LAGS[0] < NJ))
        def _():
            i, dx = job(t - LAGS[0])
            s = ychunk(i)
            a2(i, dx, 0).wait_recv()
            a2(i, dx, 1).wait_recv()
            pb[s, :, dx, 0] = total(pb[s, :, dx, 0], ry2[i, dx, 0], ry2[i, dx, 1])

        def stage(n, fn):
            u = t - EARLY - n
            near = jnp.logical_and(u >= 0, u < EARLY)
            i = jnp.where(near, u, (u + EARLY - 1) // 2)
            far = jnp.logical_and((u + EARLY - 1) % 2 == 0, jnp.logical_and(u > EARLY, i < NY))

            @pl.when(jnp.logical_or(near, far))
            def _():
                fn(i)

        def go_x(i):
            for n in range(3):
                a3(i, n).start()

        def go_z1(i):
            s = ychunk(i)
            for n in range(3):
                a3(i, n).wait_recv()
            tz[s, 0:4] = total(pb[s, lo, 0, 0], rx[i, 0], rx[i, 1], rx[i, 2]).reshape(4, 32, HW)
            z1(s)

        def sum_z(s):
            z1_done(s).wait_recv()
            fz[s] = total(tz[s, zi], tz[s, 4], tz[s, 5], tz[s, 6])
            z2(s)

        def go_z2(i):
            sum_z(ychunk(i))

        def go_z3(i):
            z3(ychunk(i))

        def x_first(i):
            s = XFIRST + i
            dw.ready(s)
            down(s, 1)
            b1(i, 1).start()
            b1(i, 2).start()
            down(s, 0)
            b1(i, 0).start()

        def x_sum(i):
            s = XFIRST + i
            for n in range(3):
                b1(i, n).wait_recv()
            for r in (3, 1, 2, 0):
                pb[s, lo, 0, r] = total(pb[s, lo, 0, r], qx[i, 0, r], qx[i, 1, r], qx[i, 2, r])
                if r == 3:
                    b2(i, 0).start()
                    b2(i, 1).start()

        def x_y2(i):
            s = XFIRST + i
            for d in range(2):
                b2(i, d).wait_recv()
                rows = slice(64 * d, 64 * d + 64)
                pb[s, lo, 0, 1 + d, rows] = total(pb[s, lo, 0, 1 + d, rows], qy1[i, d])
                b3(i, d).start()

        def x_z1(i):
            s = XFIRST + i
            b3(i, 0).wait_recv()
            b3(i, 1).wait_recv()
            tz[s, 0:4] = total(pb[s, lo, 0, 0], qy2[i, 0], qy2[i, 1]).reshape(4, 32, HW)
            z1(s)

        def x_z2(i):
            sum_z(XFIRST + i)

        def x_z3(i):
            z3(XFIRST + i)

        steps = (x_first, x_sum, x_y2, x_z1, x_z2, x_z3)
        stage(LAGS[0], go_x)
        stage(LAGS[1], go_z1)
        stage(LAGS[2], go_z2)
        stage(LAGS[3], go_z3)
        for i in range(NX):
            for fn, when in zip(steps, XTICKS[i]):
                @pl.when(t == when)
                def _(fn=fn, i=i):
                    fn(i)

        @pl.when(t == 0)
        def _():
            relay_down(2)

        @pl.when(jnp.logical_and(t >= 3, t < 6))
        def _():
            relay_down(t)

    loop(NT, r_tick)

    def drain(s):
        gw.drain(s)
        dw.drain(s)
        for d in range(2):
            s1(s, d).wait_send()
            s2(s, d).wait_send()
        og(s, 0).wait_send()
        ig(s, 0).wait_send()

        @pl.when(s < LAST)
        def _():
            for n in range(1, 3):
                og(s, n).wait_send()
                ig(s, n).wait_send()

        z1_done(s).wait_send()
        z2_done(s).wait_send()
        for par in range(2):
            cross(s, par).wait_send()
            cross(s, par).wait_recv()

    loop(NS, drain)

    def drain_y(i):
        for n in range(3):
            a3(i, n).wait_send()
        for dx in range(2):
            for d in range(2):
                a1(i, dx, d).wait_send()
                a2(i, dx, d).wait_send()

    def drain_x(i):
        for n in range(3):
            b1(i, n).wait_send()
        for d in range(2):
            b2(i, d).wait_send()
            b3(i, d).wait_send()

    loop(NY, drain_y)
    loop(NX, drain_x)
    for d in range(2):
        p1(d).wait_send()
        p2(d).wait_send()
    for n in range(2):
        ex(n, 0).wait_send()
        ex(n, 1).wait_send()


def on_device(tokens, routes, route_weights, w_gate, w_down):
    ids = jnp.arange(EXPERTS, dtype=jnp.int32)[:, None, None]
    wt = jnp.sum(jnp.where(routes.T[None] == ids, route_weights.T[None], 0.0), 1)
    dma = pltpu.SemaphoreType.DMA
    sems = (
        [dma((NS, 2))] + [dma((NS,))] * 14 + [dma, dma]
        + [dma((NS, 2))] * 4 + [dma((2,))] * 4 + [dma((NS, 3))] * 4 + [dma((2, 2))] * 2
        + [dma((NY, 2, 2))] * 4 + [dma((NY, 3))] * 2
        + [dma((NX, 3))] * 2 + [dma((NX, 2))] * 4
        + [dma((NS,))] * 5 + [dma((NS, 2))] * 2
    )
    return pl.pallas_call(
        kernel,
        out_shape=jax.ShapeDtypeStruct((ROWS, D), BF),
        in_specs=[pl.BlockSpec(memory_space=pltpu.VMEM)] + [pl.BlockSpec(memory_space=pl.ANY)] * 3,
        out_specs=pl.BlockSpec(memory_space=pl.ANY),
        scratch_shapes=[
            pltpu.VMEM((NS, 2, 2, 4, ROWS, HW), BF),
            pltpu.VMEM((NS, 2, 2, 4, ROWS, HW), BF),
            pltpu.VMEM((NS, 4, FFP, CW), BF),
            pltpu.VMEM((NS, 4, FFP, CW), BF),
            pltpu.VMEM((2, 8 * ROWS, PAIR), F32),
            pltpu.VMEM((2, 8, CAP, PAIR), BF),
            pltpu.VMEM((2, 8, CAP, PAIR), BF),
            pltpu.VMEM((8 * ROWS, 2 * PAIR), BF),
            pltpu.VMEM((8, EXPERTS, ROWS), F32),
            pltpu.VMEM((8, 2, CAP, ROWS), BF),
            pltpu.VMEM((NY, 2, 2, ROWS, HW), BF),
            pltpu.VMEM((NY, 2, 2, 2, ROWS, HW), BF),
            pltpu.VMEM((NY, 3, ROWS, HW), BF),
            pltpu.VMEM((NX, 3, 4, ROWS, HW), BF),
            pltpu.VMEM((NX, 2, ROWS // 2, HW), BF),
            pltpu.VMEM((NX, 2, ROWS, HW), BF),
            pltpu.VMEM((NS, 7, 32, HW), BF),
            pltpu.VMEM((NS, 32, HW), BF),
        ] + sems,
        compiler_params=pltpu.CompilerParams(
            collective_id=0, has_side_effects=True, vmem_limit_bytes=58 << 20
        ),
        cost_estimate=pl.CostEstimate(
            flops=8 * 8 * ROWS * FF * D, bytes_accessed=4 * FF * D * 2, transcendentals=32 * ROWS * FF
        ),
        name="moe",
    )(wt, tokens, w_gate, w_down)


def solution(mesh):
    in_specs = (
        P("expert", None),
        P("expert", None),
        P("expert", None),
        P("expert", "cuts", None),
        P("expert", "cuts", None),
    )
    return jax.shard_map(
        on_device, mesh=mesh, in_specs=in_specs, out_specs=P("expert", None), check_vma=False
    )
```
